32 devices in a mesh: seq: 4 (over z), mp: 4 (over y, core), dp: 2 (over x).
Axes of the slice: x: 2, y: 2, z: 4, core: 2. Of those that a mesh axis runs over, the one named last changes fastest.
Arguments:
- residual_in: bfloat16 [3072, 2048], P(('dp', 'seq')), parts along dimension 0, may hold values from -6 to 6
- queries: bfloat16 [3072, 2048], P(('dp', 'seq'), 'mp'), parts along dimension 0, may hold values from -30 to 30
- keys: bfloat16 [3072, 2048], P(('dp', 'seq'), 'mp'), parts along dimension 0, may hold values from -10 to 10
- values: bfloat16 [3072, 2048], P(('dp', 'seq'), 'mp'), parts along dimension 0, may hold values from -6 to 6
- w_out: bfloat16 [2048, 2048], P('mp', 'seq'), may hold values from -0.1875 to 0.1875
- conv_value: bfloat16 [2048, 2048], P('seq', 'mp'), may hold values from -0.125 to 0.125
- conv_gate: bfloat16 [2048, 2048], P('seq', 'mp'), may hold values from -0.125 to 0.125
- depth_kernel: float32 [31, 2048], P(None, 'mp'), may hold values from -2 to 2
- conv_out: bfloat16 [2048, 2048], P('mp', 'seq'), may hold values from -0.25 to 0.25
- ffn_in: bfloat16 [2048, 8192], P('seq', 'mp'), may hold values from -0.125 to 0.125
- ffn_down: bfloat16 [8192, 2048], P('mp', 'seq'), may hold values from -0.1875 to 0.1875
- ffn_mask: int32 [24, 64], P(('dp', 'seq'), 'mp'), parts along dimension 0, may hold values 0 or 1
Outputs:
- block_out: float32 [3072, 2048], P(('dp', 'seq', 'mp')), parts along dimension 0
The draws below stay inside these ranges and needn't reach their ends.
There are 2 independent parts, one for each index of `dp`. The reference program is written for one: setup_inputs(seed, part) draws one part's arguments, and reference() takes and returns one part's arrays. A program takes and returns all parts, laid end to end along the dimension named above; an argument that names none is the same for every part. Nothing has to cross between parts.
All inputs are finite; a program needn't handle non-finite values. No bound on the sum of `ffn_mask` on one device may be relied on, other than what follows from the above.
Results may differ from the reference program's by a relative error of at most 0.017.
Values may be sent and summed in bfloat16 or wider, within the bound.
No kernel may reach another device: no remote copies, remote signals or barrier semaphores. Data moves between devices by JAX's collectives and lax.ppermute only.
A program may use at most 128 MiB of HBM per device.

```python
import math
import jax
import jax.numpy as jnp
from jax import lax

HEADS = 16
HEAD_DIM = 128
FF = 8192
KERNEL = 31
TILE = 128
CBLOCK = 128
TOK_DEV = 384
D = 2048
FRAMES = 1536
N_MP = 4


def draw_queries(key, part):
    noise_key = jax.random.fold_in(key, 1)
    result = jnp.clip(1.7320508 * jax.random.normal(noise_key, (FRAMES, D), jnp.float32), -10.0, 10.0)
    return result.astype(jnp.bfloat16)


def draw_keys(key, part):
    noise_key = jax.random.fold_in(key, 2)
    result = jnp.clip(1.7320508 * jax.random.normal(noise_key, (FRAMES, D), jnp.float32), -10.0, 10.0)
    return result.astype(jnp.bfloat16)


def touch_ends(array, stream_key, least, high):
    extent = array.shape
    spot = [jax.random.randint(jax.random.fold_in(stream_key, axis), (), 0, extent[axis]) for axis in range(len(extent))]
    array = array.at[tuple(spot)].set(least)
    longest = extent.index(max(extent))
    spot[longest] = (spot[longest] + 1) % extent[longest]
    return array.at[tuple(spot)].set(high)


def levels(stream_key, shape, cuts, low, largest):
    factor_of, own = 1.0, jax.random.fold_in(stream_key, 6)
    for dim, blocks in cuts:
        steps = jnp.exp(jax.random.uniform(jax.random.fold_in(own, dim), (blocks,), jnp.float32, low / len(cuts), largest / len(cuts)))
        factor_of = factor_of * jnp.repeat(steps, shape[dim] // blocks).reshape([-1 if axis == dim else 1 for axis in range(len(shape))])
    return factor_of


def gaussian(own_key, extent, width, reach, cuts=(), held_as=jnp.bfloat16):
    values = width * jax.random.normal(own_key, extent, jnp.float32)
    if cuts:
        values = values * levels(own_key, extent, cuts, -0.22, 0.18)
    return jnp.clip(values, -reach, reach).astype(held_as)


def setup_inputs(seed: int = 0, part: int = 0) -> dict:
    seeds = jax.random.split(jax.random.key(seed), 13)
    part_keys = jax.random.split(jax.random.fold_in(seeds[12], part), 13)
    return {
        "residual_in": gaussian(part_keys[0], (FRAMES, D), 1.0, 6.0, ((0, 4),)),
        "queries": draw_queries(jax.random.fold_in(jax.random.fold_in(seeds[12], part), 71), part),
        "keys": draw_keys(jax.random.fold_in(jax.random.fold_in(seeds[12], part), 71), part),
        "values": gaussian(part_keys[3], (FRAMES, D), 1.0, 6.0, ((0, 4), (1, 4))),
        "w_out": gaussian(seeds[4], (D, D), (D // 2) ** -0.5, 0.1875, ((0, 4), (1, 4))),
        "conv_value": gaussian(seeds[5], (D, D), D ** -0.5, 0.125, ((0, 4), (1, 4))),
        "conv_gate": gaussian(seeds[6], (D, D), D ** -0.5, 0.125, ((0, 4), (1, 4))),
        "depth_kernel": gaussian(seeds[7], (KERNEL, D), (KERNEL // 4) ** -0.5, 2.0, ((1, 4),), jnp.float32),
        "conv_out": gaussian(seeds[8], (D, D), (D // 4) ** -0.5, 0.25, ((0, 4), (1, 4))),
        "ffn_in": gaussian(seeds[9], (D, FF), D ** -0.5, 0.125, ((0, 4), (1, 4))),
        "ffn_down": gaussian(seeds[10], (FF, D), (FF // 8) ** -0.5, 0.1875, ((0, 4), (1, 4))),
        "ffn_mask": touch_ends((jax.random.randint(part_keys[11], (FRAMES // TILE, FF // CBLOCK), 0, 2) < 1).astype(jnp.int32), jax.random.fold_in(part_keys[11], 1), 0, 1),
    }


def layer_norm(stream):
    row_mean = lax.optimization_barrier(jnp.mean(stream, axis=-1, keepdims=True))
    centered = stream - row_mean
    spread = lax.optimization_barrier(jnp.mean(centered * centered, axis=-1, keepdims=True))
    return centered * lax.rsqrt(spread + 1e-05)

def rounded(product):
    return lax.optimization_barrier(product.astype(jnp.bfloat16)).astype(jnp.float32)

def grouped_sum(left, weight):
    group_width = left.shape[1] // N_MP
    summed = jnp.zeros((left.shape[0], weight.shape[1]), jnp.float32)
    for group in range(N_MP):
        first_col = group * group_width
        product = jnp.dot(left[:, first_col:first_col + group_width], weight[first_col:first_col + group_width], preferred_element_type=jnp.float32)
        summed = summed + rounded(product)
    return summed

def attention(queries, keys, values):
    score_scale = 1.0 / math.sqrt(HEAD_DIM)
    key_heads = keys.astype(jnp.float32).reshape(FRAMES, HEADS, HEAD_DIM)
    value_heads = values.astype(jnp.float32).reshape(FRAMES, HEADS, HEAD_DIM)
    query_blocks = queries.astype(jnp.float32).reshape(FRAMES // TOK_DEV, TOK_DEV, HEADS, HEAD_DIM)

    def one_block(query_heads):
        scores = jnp.einsum('qhd,khd->qhk', query_heads, key_heads) * score_scale
        row_max = lax.optimization_barrier(jnp.max(scores, axis=-1, keepdims=True))
        exp_scores = jnp.exp(scores - row_max)
        row_sum = lax.optimization_barrier(jnp.sum(exp_scores, axis=-1))
        probs = lax.optimization_barrier(exp_scores.astype(jnp.bfloat16)).astype(jnp.float32)
        mixed = jnp.einsum('qhk,khd->qhd', probs, value_heads)
        return (mixed / row_sum[..., None]).astype(jnp.bfloat16)
    return lax.map(one_block, query_blocks).reshape(FRAMES, HEADS * HEAD_DIM)

def reference(residual_in, queries, keys, values, w_out, conv_value, conv_gate, depth_kernel, conv_out, ffn_in, ffn_down, ffn_mask):
    heads_out = attention(queries, keys, values)
    stream_one = residual_in.astype(jnp.float32) + grouped_sum(heads_out, w_out)
    norm_one = layer_norm(stream_one).astype(jnp.bfloat16)
    value_half = jnp.dot(norm_one, conv_value, preferred_element_type=jnp.float32)
    gate_half = jnp.dot(norm_one, conv_gate, preferred_element_type=jnp.float32)
    gated_units = (value_half * jax.nn.sigmoid(gate_half)).astype(jnp.bfloat16)
    half_width = KERNEL // 2
    padded = jnp.pad(gated_units, ((half_width, half_width), (0, 0)))
    depth_out = jnp.zeros((FRAMES, D), jnp.float32)
    for tap_index in range(KERNEL):
        depth_out = depth_out + depth_kernel[tap_index] * padded[tap_index:tap_index + FRAMES].astype(jnp.float32)
    activated = jax.nn.silu(depth_out).astype(jnp.bfloat16)
    stream_two = stream_one + grouped_sum(activated, conv_out)
    norm_two = layer_norm(stream_two).astype(jnp.bfloat16)
    pre_hidden = jnp.dot(norm_two, ffn_in, preferred_element_type=jnp.float32)
    gate_table = jnp.repeat(jnp.repeat(ffn_mask, TILE, axis=0), CBLOCK, axis=1).astype(jnp.float32)
    hidden = (jax.nn.silu(pre_hidden) * gate_table).astype(jnp.bfloat16)
    stream_three = stream_two + 0.5 * grouped_sum(hidden, ffn_down)
    return layer_norm(stream_three)
```

```python
import math

import jax
import jax.numpy as jnp
from jax import lax
from jax.sharding import PartitionSpec as P

HEAD_DIM = 128


norm_epsilon = 1e-05


def ring_pairs(axis):
    count = lax.axis_size(axis)
    return [(i, (i + 1) % count) for i in range(count)]


class Lane:
    def __init__(self, axis, depth):
        self.axis, self.depth, self.ended = axis, depth, []

    def step(self, value):
        if len(self.ended) >= self.depth:
            value, _ = lax.optimization_barrier((value, self.ended[-self.depth]))
        value = lax.ppermute(value, self.axis, ring_pairs(self.axis))
        self.ended.append(value)
        return value


def rings(lane, starts):
    held = [[start] for start in starts]
    for _ in range(lax.axis_size(lane.axis) - 1):
        for pieces in held:
            pieces.append(lane.step(pieces[-1]))
    return held


def part_of(weight, dim, index):
    width = weight.shape[dim] // lax.axis_size("dp")
    return lax.dynamic_slice_in_dim(weight, index * width, width, axis=dim)


def spread(lane, weights):
    part_count = lax.axis_size("dp")
    here = lax.axis_index("dp")
    fetched = rings(lane, [part_of(weight, dim, here) for weight, dim in weights])
    result = []
    for (weight, dim), pieces in zip(weights, fetched):
        parts = []
        for t, piece in enumerate(pieces):
            parts.append(piece)
            for p in range(1, part_count):
                if t == 0:
                    piece = part_of(weight, dim, (here - p) % part_count)
                else:
                    piece = lax.ppermute(piece, "dp", ring_pairs("dp"))
                parts.append(piece)
        result.append(parts)
    return result


def to_held_order(value):
    count, part_count = lax.axis_size("seq"), lax.axis_size("dp")
    s, h = lax.axis_index("seq"), lax.axis_index("dp")
    width = value.shape[1] // (count * part_count)
    return jnp.concatenate(
        [
            lax.dynamic_slice_in_dim(
                value, ((s - t) % count * part_count + (h - p) % part_count) * width, width, axis=1
            )
            for t in range(count)
            for p in range(part_count)
        ],
        axis=1,
    )


def to_natural_order(value):
    count, part_count = lax.axis_size("seq"), lax.axis_size("dp")
    s, h = lax.axis_index("seq"), lax.axis_index("dp")
    width = value.shape[1] // (count * part_count)
    return jnp.concatenate(
        [
            lax.dynamic_slice_in_dim(
                value, ((s - b) % count * part_count + (h - q) % part_count) * width, width, axis=1
            )
            for b in range(count)
            for q in range(part_count)
        ],
        axis=1,
    )


def neighbours(value, axis, width):
    count, length = (lax.axis_size(axis), value.shape[0])
    up = [(i, (i + 1) % count) for i in range(count - 1)]
    down = [(j, i) for i, j in up]
    before = lax.ppermute(value[length - width :], axis, up)
    after = lax.ppermute(value[:width], axis, down)
    return jnp.concatenate([before, value, after], axis=0)


def layer_norm(stream):
    row_mean = jnp.mean(stream, axis=-1, keepdims=True)
    centered = stream - row_mean
    spread_of = jnp.mean(centered * centered, axis=-1, keepdims=True)
    return centered * lax.rsqrt(spread_of + norm_epsilon)


def dot(left, right):
    return jnp.dot(left, right, preferred_element_type=jnp.float32)


def xor_pairs(count, bit):
    return [(i, i ^ bit) for i in range(count)]


def scatter_sum(part):
    count = lax.axis_size("mp")
    if count & (count - 1):
        return lax.psum_scatter(
            part.astype(jnp.bfloat16), "mp", scatter_dimension=0, tiled=True
        ).astype(jnp.float32)
    me = lax.axis_index("mp")
    bit = 1
    while bit < count:
        groups = part.reshape(count // (2 * bit), 2, -1, part.shape[1])
        mine = (me // bit) % 2
        sent = lax.dynamic_index_in_dim(groups, 1 - mine, 1, keepdims=False).astype(jnp.bfloat16)
        kept = lax.dynamic_index_in_dim(groups, mine, 1, keepdims=False)
        taken = lax.ppermute(sent, "mp", xor_pairs(count, bit))
        part = (kept + taken.astype(jnp.float32)).reshape(-1, part.shape[1])
        bit *= 2
    return part


def widen(rows):
    count = lax.axis_size("mp")
    if count & (count - 1):
        return lax.all_gather(rows, "mp", axis=0, tiled=True)
    me = lax.axis_index("mp")
    share, width = rows.shape
    bit = count // 2
    held = rows[None]
    while bit:
        taken = lax.ppermute(held, "mp", xor_pairs(count, bit))
        first = (me // bit) % 2 == 0
        held = jnp.stack(
            [jnp.where(first, held, taken), jnp.where(first, taken, held)], axis=1
        ).reshape(-1, share, width)
        bit //= 2
    return held.reshape(count * share, width)


def attention(queries, keys, values):
    row_count, local_width = queries.shape
    heads_here = local_width // HEAD_DIM
    query_heads = queries.reshape(row_count, heads_here, HEAD_DIM)
    key_heads = keys.reshape(-1, heads_here, HEAD_DIM)
    value_heads = values.reshape(-1, heads_here, HEAD_DIM)
    scores = jnp.einsum(
        "qhd,khd->qhk", query_heads, key_heads, preferred_element_type=jnp.float32
    ) * (1.0 / math.sqrt(HEAD_DIM))
    exp_scores = jnp.exp(scores - jnp.max(scores, axis=-1, keepdims=True))
    total = jnp.sum(exp_scores, axis=-1)
    weighted = jnp.einsum(
        "qhk,khd->qhd",
        exp_scores.astype(jnp.bfloat16),
        value_heads,
        preferred_element_type=jnp.float32,
    )
    return (weighted / total[..., None]).reshape(row_count, local_width).astype(jnp.bfloat16)


def on_device(
    residual_in,
    queries,
    keys,
    values,
    w_out,
    conv_value,
    conv_gate,
    depth_kernel,
    conv_out,
    ffn_in,
    ffn_down,
    ffn_mask,
):
    row_count = queries.shape[0]
    lane = Lane("seq", 2)
    key_pieces, value_pieces = rings(lane, [keys, values])
    (w_out_parts, value_parts, gate_parts) = spread(
        lane, [(w_out, 1), (conv_value, 0), (conv_gate, 0)]
    )
    half = ffn_in.shape[1] // 2
    conv_out_parts, in_parts_a, in_parts_b = spread(
        lane, [(conv_out, 1), (ffn_in[:, :half], 0), (ffn_in[:, half:], 0)]
    )
    down_parts_a, down_parts_b = spread(lane, [(ffn_down[:half], 1), (ffn_down[half:], 1)])

    heads_out = attention(
        queries, jnp.concatenate(key_pieces, axis=0), jnp.concatenate(value_pieces, axis=0)
    )
    attn_part = jnp.concatenate([dot(heads_out, part) for part in w_out_parts], axis=1)
    share_count = row_count // lax.axis_size("mp")
    stream = to_held_order(
        lax.dynamic_slice_in_dim(
            residual_in, lax.axis_index("mp") * share_count, share_count, 0
        )
    ).astype(jnp.float32)
    stream = stream + scatter_sum(attn_part)
    norm_one = widen(layer_norm(stream).astype(jnp.bfloat16))

    def through(normed, parts):
        width = parts[0].shape[0]
        return sum(
            dot(normed[:, i * width : (i + 1) * width], part) for i, part in enumerate(parts)
        )

    value_half = through(norm_one, value_parts)
    gate_half = through(norm_one, gate_parts)
    gated_units = (value_half * jax.nn.sigmoid(gate_half)).astype(jnp.bfloat16)
    padded = neighbours(gated_units, "seq", depth_kernel.shape[0] // 2)
    depth_out = jnp.zeros(gated_units.shape, jnp.float32)
    for tap_index in range(depth_kernel.shape[0]):
        depth_out = depth_out + depth_kernel[tap_index] * padded[
            tap_index : tap_index + row_count
        ].astype(jnp.float32)
    activated = jax.nn.silu(depth_out).astype(jnp.bfloat16)
    conv_part = jnp.concatenate([dot(activated, part) for part in conv_out_parts], axis=1)
    stream = stream + scatter_sum(conv_part)
    norm_two = widen(layer_norm(stream).astype(jnp.bfloat16))

    tile_count, block_count = ffn_mask.shape

    def hidden_of(parts, mask):
        pre_hidden = through(norm_two, parts)
        hidden = (
            jax.nn.silu(pre_hidden).reshape(
                tile_count, row_count // tile_count, mask.shape[1], -1
            )
            * mask.astype(jnp.float32)[:, None, :, None]
        )
        return hidden.reshape(row_count, -1).astype(jnp.bfloat16)

    hidden_a = hidden_of(in_parts_a, ffn_mask[:, : block_count // 2])
    hidden_b = hidden_of(in_parts_b, ffn_mask[:, block_count // 2 :])
    ffn_part = jnp.concatenate(
        [dot(hidden_a, a) + dot(hidden_b, b) for a, b in zip(down_parts_a, down_parts_b)], axis=1
    )
    stream = stream + 0.5 * scatter_sum(ffn_part)
    return to_natural_order(layer_norm(stream))


def solution(mesh):
    in_specs = (
        P(("dp", "seq"), None),
        P(("dp", "seq"), "mp"),
        P(("dp", "seq"), "mp"),
        P(("dp", "seq"), "mp"),
        P("mp", "seq"),
        P("seq", "mp"),
        P("seq", "mp"),
        P(None, "mp"),
        P("mp", "seq"),
        P("seq", "mp"),
        P("mp", "seq"),
        P(("dp", "seq"), "mp"),
    )
    out_specs = P(("dp", "seq", "mp"), None)
    return jax.shard_map(
        on_device, mesh=mesh, in_specs=in_specs, out_specs=out_specs, check_vma=False
    )
```

```python
import functools
import math

import jax
import jax.numpy as jnp
from jax import lax
from jax.experimental import pallas as pl
from jax.experimental.pallas import tpu as pltpu
from jax.sharding import PartitionSpec as P

HEAD_DIM = 128


norm_epsilon = 1e-05


def ring_pairs(axis):
    count = lax.axis_size(axis)
    return [(i, (i + 1) % count) for i in range(count)]


class Line:
    def __init__(self, depth):
        self.depth, self.waiting, self.under_way, self.crossing = depth, [], [], []
        self.parts = {}

    def add(self, weights):
        for t in range(1, lax.axis_size("seq")):
            for name, array, dim in weights:
                self.waiting.append((name, t, dim))
                if t == 1:
                    self.parts[name, 0] = own_parts(array, dim)

    def start(self):
        if not self.waiting:
            return
        name, t, dim = self.waiting[0]
        if (name, t - 1) not in self.parts:
            return
        del self.waiting[0]
        piece = self.parts[name, t - 1][0]
        if self.token is not None:
            piece, _ = lax.optimization_barrier((piece, self.token))
        self.under_way.append((name, t, dim, lax.ppermute(piece, "seq", ring_pairs("seq"))))

    def begin(self):
        self.token = None
        while len(self.under_way) < self.depth:
            self.start()

    def visit(self, *beside):
        crossed = None
        if self.under_way:
            name, t, dim, piece = self.under_way.pop(0)
            if len(self.crossing) > 1:
                crossed = self.crossing.pop(0)
                (beside, piece, taken) = lax.optimization_barrier((beside, piece, crossed[2]))
            else:
                (beside, piece) = lax.optimization_barrier((beside, piece))
            self.token = piece
            parts = [piece]
            self.parts[name, t] = parts
            while len(self.under_way) < self.depth:
                held = len(self.under_way)
                self.start()
                if len(self.under_way) == held:
                    break
            if dim is not None:
                for _ in range(1, lax.axis_size("dp")):
                    piece = lax.ppermute(piece, "dp", ring_pairs("dp"))
                    self.crossing.append((name, t, piece))
        elif self.crossing:
            crossed = self.crossing.pop(0)
            (beside, taken) = lax.optimization_barrier((beside, crossed[2]))
        if crossed is not None:
            self.parts[crossed[0], crossed[1]].append(taken)
        return beside if len(beside) != 1 else beside[0]

    def visits(self, number, beside):
        for _ in range(number * (lax.axis_size("seq") - 1) // 3):
            beside = self.visit(beside)
        return beside

    def has(self, name, first=0, last=None):
        last = lax.axis_size("seq") if last is None else last
        width = len(self.parts[name, 0])
        return all(len(self.parts.get((name, t), ())) == width for t in range(first, last))

    def until(self, names, beside, first=0, last=None):
        while not all(self.has(name, first, last) for name in names):
            beside = self.visit(beside)
        return beside

    def take(self, name, dim, first=0, last=None):
        last = lax.axis_size("seq") if last is None else last
        parts = [part for t in range(first, last) for part in self.parts[name, t]]
        if parts[0].shape[dim] % 128:
            parts = [jnp.concatenate(parts, axis=dim)]
        return parts


def part_of(weight, dim, index):
    width = weight.shape[dim] // lax.axis_size("dp")
    return lax.dynamic_slice_in_dim(weight, index * width, width, axis=dim)


def own_parts(array, dim):
    if dim is None:
        return [array]
    count, here = lax.axis_size("dp"), lax.axis_index("dp")
    return [part_of(array, dim, (here - p) % count) for p in range(count)]


def to_held_order(value):
    count, part_count = lax.axis_size("seq"), lax.axis_size("dp")
    s, h = lax.axis_index("seq"), lax.axis_index("dp")
    width = value.shape[1] // (count * part_count)
    return jnp.concatenate(
        [
            lax.dynamic_slice_in_dim(
                value, ((s - t) % count * part_count + (h - p) % part_count) * width, width, axis=1
            )
            for t in range(count)
            for p in range(part_count)
        ],
        axis=1,
    )


def to_natural_order(value):
    count, part_count = lax.axis_size("seq"), lax.axis_size("dp")
    s, h = lax.axis_index("seq"), lax.axis_index("dp")
    width = value.shape[1] // (count * part_count)
    return jnp.concatenate(
        [
            lax.dynamic_slice_in_dim(
                value, ((s - b) % count * part_count + (h - q) % part_count) * width, width, axis=1
            )
            for b in range(count)
            for q in range(part_count)
        ],
        axis=1,
    )


def layer_norm(stream):
    row_mean = jnp.mean(stream, axis=-1, keepdims=True)
    centered = stream - row_mean
    spread_of = jnp.mean(centered * centered, axis=-1, keepdims=True)
    return centered * lax.rsqrt(spread_of + norm_epsilon)


def dot(left, right):
    return jnp.dot(left, right, preferred_element_type=jnp.float32)


def xor_pairs(count, bit):
    return [(i, i ^ bit) for i in range(count)]


def scatter_sum(sent, kept, line, visits):
    count = lax.axis_size("mp")
    me = lax.axis_index("mp")
    bit = 1
    while True:
        taken = lax.ppermute(sent, "mp", xor_pairs(count, bit))
        kept = line.visits(visits[0] if bit == 1 else visits[1], kept)
        part = kept + taken.astype(jnp.float32)
        bit *= 2
        if bit == count:
            return part[0]
        groups = part.reshape(-1, 2, *part.shape[1:])
        mine = (me // bit) % 2
        sent = lax.dynamic_index_in_dim(groups, 1 - mine, 1, keepdims=False).astype(jnp.bfloat16)
        kept = lax.dynamic_index_in_dim(groups, mine, 1, keepdims=False)


def widen(rows, line, visits):
    count = lax.axis_size("mp")
    me = lax.axis_index("mp")
    share, width = rows.shape
    bit = count // 2
    held = rows[None]
    while bit:
        taken = lax.ppermute(held, "mp", xor_pairs(count, bit))
        held = line.visits(visits[1] if bit > 1 else visits[0], held)
        first = (me // bit) % 2 == 0
        held = jnp.stack(
            [jnp.where(first, held, taken), jnp.where(first, taken, held)], axis=1
        ).reshape(-1, share, width)
        bit //= 2
    return held.reshape(count * share, width)


def kernel_call(kernel, outs, args, scratch=(), scalars=0):
    return pl.pallas_call(
        kernel,
        out_shape=outs,
        in_specs=[pl.BlockSpec(memory_space=pltpu.SMEM)] * scalars
        + [pl.BlockSpec(memory_space=pltpu.VMEM)] * (len(args) - scalars),
        out_specs=jax.tree.map(lambda _: pl.BlockSpec(memory_space=pltpu.VMEM), outs),
        scratch_shapes=scratch,
        compiler_params=pltpu.CompilerParams(vmem_limit_bytes=56 * 1024 * 1024),
    )(*args)


def attention_kernel(count, q_ref, *refs):
    k_refs, v_refs, o_ref = refs[:count], refs[count : 2 * count], refs[2 * count]
    rows, width = q_ref.shape
    block = 128 if rows % 128 == 0 else rows
    scale = 1.0 / math.sqrt(HEAD_DIM)

    @pl.loop(0, rows // block)
    def _(r):
        here = pl.ds(pl.multiple_of(r * block, block), block)
        for first in range(0, width, HEAD_DIM):
            columns = slice(first, first + HEAD_DIM)
            q = q_ref[here, columns]
            scores = [
                lax.dot_general(
                    q,
                    k_ref[:, columns],
                    (((1,), (1,)), ((), ())),
                    preferred_element_type=jnp.float32,
                )
                * scale
                for k_ref in k_refs
            ]
            top = functools.reduce(
                jnp.maximum, [jnp.max(s, axis=1, keepdims=True) for s in scores]
            )
            weights = [jnp.exp(s - top) for s in scores]
            total = sum(jnp.sum(w, axis=1, keepdims=True) for w in weights)
            mixed = sum(
                dot(w.astype(jnp.bfloat16), v_ref[:, columns])
                for w, v_ref in zip(weights, v_refs)
            )
            o_ref[here, columns] = (mixed / total).astype(o_ref.dtype)


def attention(queries, key_pieces, value_pieces):
    return kernel_call(
        functools.partial(attention_kernel, len(key_pieces)),
        jax.ShapeDtypeStruct(queries.shape, jnp.bfloat16),
        (queries, *key_pieces, *value_pieces),
    )


def share_out(product_ref, sent_ref, kept_ref, columns):
    half, share = sent_ref.shape[:2]
    mine = lax.axis_index("mp") % 2
    for j in range(half):
        theirs = pl.ds(pl.multiple_of((2 * j + 1 - mine) * share, share), share)
        ours = pl.ds(pl.multiple_of((2 * j + mine) * share, share), share)
        sent_ref[j, :, columns] = product_ref[theirs, :].astype(sent_ref.dtype)
        kept_ref[j, :, columns] = product_ref[ours, :]


def project_refs(lefts, parts, sent_ref, kept_ref, product_ref):
    width = product_ref.shape[1]
    for i, blocks in enumerate(parts):
        product_ref[...] = sum(dot(left[...], block[...]) for left, block in zip(lefts, blocks))
        share_out(product_ref, sent_ref, kept_ref, slice(i * width, (i + 1) * width))


def project_kernel(left_count, *refs):
    lefts, (sent_ref, kept_ref, product_ref) = refs[:left_count], refs[-3:]
    blocks = refs[left_count:-3]
    number = len(blocks) // left_count
    project_refs(
        lefts,
        [blocks[i::number] for i in range(number)],
        sent_ref,
        kept_ref,
        product_ref,
    )


def shares(rows, columns):
    count = lax.axis_size("mp")
    shape = (count // 2, rows // count, columns)
    return (
        jax.ShapeDtypeStruct(shape, jnp.bfloat16),
        jax.ShapeDtypeStruct(shape, jnp.float32),
    )


def project(lefts, parts):
    rows, width = lefts[0].shape[0], parts[0][0].shape[1]
    return kernel_call(
        functools.partial(project_kernel, len(lefts)),
        shares(rows, width * len(parts[0])),
        (*lefts, *[block for blocks in parts for block in blocks]),
        [pltpu.VMEM((rows, width), jnp.float32)],
    )


def through(x_ref, parts, columns):
    width = parts[0].shape[0]
    return sum(
        dot(x_ref[:, i * width : (i + 1) * width], part[:, columns])
        for i, part in enumerate(parts)
    )


def column_tiles(width):
    tile = 256 if width % 256 == 0 else width
    return width // tile, tile


def gated_kernel(count, x_ref, *refs):
    value_refs, gate_refs, o_ref = refs[:count], refs[count : 2 * count], refs[2 * count]
    tiles, tile = column_tiles(o_ref.shape[1])

    @pl.loop(0, tiles)
    def _(n):
        columns = pl.ds(pl.multiple_of(n * tile, tile), tile)
        gate = through(x_ref, gate_refs, columns)
        value = through(x_ref, value_refs, columns)
        o_ref[:, columns] = (value / (1.0 + jnp.exp(-gate))).astype(o_ref.dtype)


def gated(normed, value_parts, gate_parts):
    return kernel_call(
        functools.partial(gated_kernel, len(value_parts)),
        jax.ShapeDtypeStruct((normed.shape[0], value_parts[0].shape[1]), jnp.bfloat16),
        (normed, *value_parts, *gate_parts),
    )


def conv_kernel(x_ref, before_ref, after_ref, taps_ref, *refs):
    parts, (sent_ref, kept_ref, product_ref, padded_ref, active_ref) = refs[:-5], refs[-5:]
    edge, rows = before_ref.shape[0], x_ref.shape[0]
    taps = taps_ref.shape[0]
    shift = edge - taps // 2
    padded_ref[:edge, :] = before_ref[...].astype(jnp.float32)
    padded_ref[edge : edge + rows, :] = x_ref[...].astype(jnp.float32)
    padded_ref[edge + rows :, :] = after_ref[...].astype(jnp.float32)
    block = 64 if rows % 64 == 0 else rows
    for first in range(0, x_ref.shape[1], 128):
        columns = slice(first, first + 128)

        @pl.loop(0, rows // block)
        def _(r):
            base = pl.multiple_of(r * block, block)
            window = padded_ref[pl.ds(base, block + 2 * edge), columns]
            total = jnp.zeros((block, window.shape[1]), jnp.float32)
            for t in range(taps):
                total += taps_ref[t : t + 1, columns] * window[t + shift : t + shift + block]
            active_ref[pl.ds(base, block), columns] = (total / (1.0 + jnp.exp(-total))).astype(
                jnp.bfloat16
            )

    project_refs([active_ref], [[part] for part in parts], sent_ref, kept_ref, product_ref)


def conv_branch(units, taps, parts):
    rows, channels = units.shape
    edge = -(-(taps.shape[0] // 2) // 16) * 16
    count = lax.axis_size("seq")
    up = [(i, i + 1) for i in range(count - 1)]
    down = [(j, i) for i, j in up]
    before = lax.ppermute(units[rows - edge :], "seq", up)
    after = lax.ppermute(units[:edge], "seq", down)
    width = parts[0].shape[1]
    return kernel_call(
        conv_kernel,
        shares(rows, width * len(parts)),
        (units, before, after, taps, *parts),
        [
            pltpu.VMEM((rows, width), jnp.float32),
            pltpu.VMEM((rows + 2 * edge, channels), jnp.float32),
            pltpu.VMEM((rows, channels), jnp.bfloat16),
        ],
    )


def hidden_kernel(mask_ref, x_ref, *refs):
    parts, o_ref = refs[:-1], refs[-1]
    rows, width = o_ref.shape
    tile_rows, block = rows // mask_ref.shape[0], width // mask_ref.shape[1]
    tiles, tile = column_tiles(width)

    @pl.loop(0, tiles)
    def _(n):
        units = through(x_ref, parts, pl.ds(pl.multiple_of(n * tile, tile), tile))
        units = units / (1.0 + jnp.exp(-units))
        for r in range(mask_ref.shape[0]):
            for j in range(tile // block):
                factor = mask_ref[r, n * (tile // block) + j].astype(jnp.float32)
                masked = (
                    units[r * tile_rows : (r + 1) * tile_rows, j * block : (j + 1) * block] * factor
                )
                o_ref[
                    r * tile_rows : (r + 1) * tile_rows,
                    pl.ds(pl.multiple_of(n * tile + j * block, block), block),
                ] = masked.astype(o_ref.dtype)


def hidden_of(normed, parts, mask):
    return kernel_call(
        hidden_kernel,
        jax.ShapeDtypeStruct((normed.shape[0], parts[0].shape[1]), jnp.bfloat16),
        (mask, normed, *parts),
        scalars=1,
    )


def on_device(
    residual_in,
    queries,
    keys,
    values,
    w_out,
    conv_value,
    conv_gate,
    depth_kernel,
    conv_out,
    ffn_in,
    ffn_down,
    ffn_mask,
):
    row_count = queries.shape[0]
    half = ffn_in.shape[1] // 2
    line = Line(3)
    line.add([("keys", keys, None), ("values", values, None), ("w_out", w_out, 1)])
    line.add([("value", conv_value, 0), ("gate", conv_gate, 0), ("conv_out", conv_out, 1)])
    line.add([("in_a", ffn_in[:, :half], 0), ("in_b", ffn_in[:, half:], 0)])
    line.add([("down_a", ffn_down[:half], 1), ("down_b", ffn_down[half:], 1)])
    line.begin()

    share_count = row_count // lax.axis_size("mp")
    stream = to_held_order(
        lax.dynamic_slice_in_dim(
            residual_in, lax.axis_index("mp") * share_count, share_count, 0
        )
    )
    queries = line.until(["keys", "values"], queries)
    heads_out = attention(queries, line.take("keys", 0), line.take("values", 0))
    heads_out = line.until(["w_out"], heads_out)
    sent, kept = project([heads_out], [line.take("w_out", 1)])
    stream = stream.astype(jnp.float32) + scatter_sum(sent, kept, line, (1, 2))
    norm_one = widen(layer_norm(stream).astype(jnp.bfloat16), line, (1, 2))

    norm_one = line.until(["value", "gate"], norm_one)
    units = gated(norm_one, line.take("value", 0), line.take("gate", 0))
    units = line.until(["conv_out"], units)
    sent, kept = conv_branch(units, depth_kernel, line.take("conv_out", 1))
    stream = stream + scatter_sum(sent, kept, line, (1, 1))
    norm_two = widen(layer_norm(stream).astype(jnp.bfloat16), line, (1, 1))

    blocks = ffn_mask.shape[1] // 2
    norm_two = line.until(["in_a"], norm_two)
    hidden_a = hidden_of(norm_two, line.take("in_a", 0), ffn_mask[:, :blocks])
    norm_two, hidden_a = line.until(["in_b"], (norm_two, hidden_a))
    hidden_b = hidden_of(norm_two, line.take("in_b", 0), ffn_mask[:, blocks:])
    hidden = line.until(["down_a", "down_b"], (hidden_a, hidden_b))
    sent, kept = project(hidden, [line.take("down_a", 1), line.take("down_b", 1)])
    stream = stream + 0.5 * scatter_sum(sent, kept, line, (0, 0))
    return to_natural_order(layer_norm(stream))


def solution(mesh):
    in_specs = (
        P(("dp", "seq"), None),
        P(("dp", "seq"), "mp"),
        P(("dp", "seq"), "mp"),
        P(("dp", "seq"), "mp"),
        P("mp", "seq"),
        P("seq", "mp"),
        P("seq", "mp"),
        P(None, "mp"),
        P("mp", "seq"),
        P("seq", "mp"),
        P("mp", "seq"),
        P(("dp", "seq"), "mp"),
    )
    out_specs = P(("dp", "seq", "mp"), None)
    return jax.shard_map(
        on_device, mesh=mesh, in_specs=in_specs, out_specs=out_specs, check_vma=False
    )
```

```python
import functools
import math

import jax
import jax.numpy as jnp
from jax import lax
from jax.experimental import pallas as pl
from jax.experimental.pallas import tpu as pltpu
from jax.sharding import PartitionSpec as P

HEAD_DIM = 128


norm_epsilon = 1e-05


def ring_pairs(axis):
    count = lax.axis_size(axis)
    return [(i, (i + 1) % count) for i in range(count)]


class Rows:
    def __init__(self, array, first, count, block=None):
        self.array, self.first, self.count, self.block = array, first, count, block
        self.shape = (count, array.shape[1])

    def __getitem__(self, columns):
        if self.block is None:
            return self.array[self.first : self.first + self.count, columns]
        t, rows = self.block
        size = lax.axis_size("seq")
        start = lax.rem(lax.axis_index("seq") + (size - t), size) * rows + self.first
        return self.array[pl.ds(pl.multiple_of(start, math.gcd(rows, self.first)), self.count), columns]


class Line:
    def __init__(self, depth, lag):
        self.depth, self.lag = depth, lag
        self.waiting, self.under_way, self.crossing = [], [], []
        self.parts, self.pieces, self.token = {}, {}, None

    def add(self, first, last, *stream):
        by_width = {}
        for name, array in stream:
            self.parts[name, 0] = [Rows(array, 0, array.shape[0])]
            by_width.setdefault(array.shape[1], []).append((name, array))
        count, here = lax.axis_size("dp"), lax.axis_index("dp")
        steps = lax.axis_size("seq") - 1
        for held in by_width.values():
            fields = tuple((name, array.shape[0] // count) for name, array in held)
            own = [
                lax.dynamic_slice_in_dim(array, here * rows, rows, axis=0)
                for (_, array), (_, rows) in zip(held, fields)
            ]
            self.pieces[fields, 0] = own[0] if len(own) == 1 else jnp.concatenate(own, axis=0)
            for t in range(1, steps + 1):
                place = first + (last - first) * (t - 1) / max(steps - 1, 1)
                self.waiting.append((place, fields, t))

    def begin(self):
        self.waiting.sort(key=lambda step: step[0])
        self.refill()

    def refill(self):
        while self.waiting and len(self.under_way) < self.depth:
            _, fields, t = self.waiting[0]
            if (fields, t - 1) not in self.pieces:
                return
            del self.waiting[0]
            piece = self.pieces[fields, t - 1]
            if self.token is not None:
                piece, _ = lax.optimization_barrier((piece, self.token))
            self.under_way.append((fields, t, lax.ppermute(piece, "seq", ring_pairs("seq"))))

    def note(self, fields, t, piece):
        first = 0
        for name, rows in fields:
            self.parts.setdefault((name, t), []).append(Rows(piece, first, rows))
            first += rows

    def visit(self, beside):
        lag = self.lag if self.under_way else 0
        taken = self.crossing.pop(0) if len(self.crossing) > lag else None
        crossed = taken[2] if taken else None
        if self.under_way:
            fields, t, piece = self.under_way.pop(0)
            beside, piece, crossed = lax.optimization_barrier((beside, piece, crossed))
            self.token = self.pieces[fields, t] = piece
            self.note(fields, t, piece)
            self.refill()
            for _ in range(1, lax.axis_size("dp")):
                piece = lax.ppermute(piece, "dp", ring_pairs("dp"))
                self.crossing.append((fields, t, piece))
        else:
            beside, crossed = lax.optimization_barrier((beside, crossed))
        if taken:
            self.note(taken[0], taken[1], crossed)
        return beside

    def cross(self, beside):
        fields, t, taken = self.crossing.pop(0)
        beside, taken = lax.optimization_barrier((beside, taken))
        self.note(fields, t, taken)
        return beside

    def visits(self, number, beside):
        for _ in range(number * (lax.axis_size("seq") - 1) // 3):
            beside = self.visit(beside)
        return beside

    def until(self, names, beside, first=0, last=None):
        last = lax.axis_size("seq") if last is None else last
        wanted = [(name, t) for name in names for t in range(max(first, 1), last)]
        while any(len(self.parts.get(key, ())) < lax.axis_size("dp") for key in wanted):
            arrived = all(key in self.parts for key in wanted)
            beside = self.cross(beside) if arrived else self.visit(beside)
        return beside

    def take(self, name, first=0, last=None):
        last = lax.axis_size("seq") if last is None else last
        here, count = lax.axis_index("dp"), lax.axis_size("dp")
        blocks = []
        for t in range(first, last):
            parts = self.parts[name, t]
            if len(parts) > 1 and parts[0].shape[0] % 128:
                held = jnp.stack([part[:] for part in parts])
                whole = jnp.concatenate(
                    [
                        lax.dynamic_index_in_dim(held, (here - q) % count, 0, keepdims=False)
                        for q in range(count)
                    ],
                    axis=0,
                )
                parts = [Rows(whole, 0, whole.shape[0])]
            blocks.append(parts)
        return blocks


class Gathered:
    def __init__(self, token, array):
        self.rows = array.shape[0]
        if token is not None:
            array, _ = lax.optimization_barrier((array, token))
        self.array = lax.all_gather(array, "seq", axis=0, tiled=True)

    def end(self, beside):
        beside, self.array = lax.optimization_barrier((beside, self.array))
        return beside

    def take(self):
        return [
            [Rows(self.array, 0, self.rows, (t, self.rows))] for t in range(lax.axis_size("seq"))
        ]


def packed(weights):
    arrays, places = [], {}

    def place(item):
        if isinstance(item, list):
            return [place(inner) for inner in item]
        if id(item.array) not in places:
            places[id(item.array)] = len(arrays)
            arrays.append(item.array)
        return places[id(item.array)], item.first, item.count, item.block

    spec = place(weights)
    return arrays, spec


def unpacked(spec, refs):
    if isinstance(spec, list):
        return [unpacked(inner, refs) for inner in spec]
    return Rows(refs[spec[0]], *spec[1:])


def layer_norm(stream):
    row_mean = jnp.mean(stream, axis=-1, keepdims=True)
    centered = stream - row_mean
    spread_of = jnp.mean(centered * centered, axis=-1, keepdims=True)
    return centered * lax.rsqrt(spread_of + norm_epsilon)


def dot(left, right):
    return jnp.dot(left, right, preferred_element_type=jnp.float32)


def xor_pairs(count, bit):
    return [(i, i ^ bit) for i in range(count)]


def fenced(function, *values):
    outs = jax.eval_shape(function, *values)
    return lax.cond(
        lax.axis_index("seq") < lax.axis_size("seq"),
        function,
        lambda *_: jax.tree.map(lambda out: jnp.zeros(out.shape, out.dtype), outs),
        *values,
    )


def scatter_sum(sent, kept):
    count = lax.axis_size("mp")
    me = lax.axis_index("mp")
    bit = 1
    while True:
        taken = lax.ppermute(sent, "mp", xor_pairs(count, bit))
        bit *= 2
        if bit == count:
            return kept[0], taken[0]
        part = kept + taken.astype(jnp.float32)
        groups = part.reshape(-1, 2, *part.shape[1:])
        mine = (me // bit) % 2
        sent = lax.dynamic_index_in_dim(groups, 1 - mine, 1, keepdims=False).astype(jnp.bfloat16)
        kept = lax.dynamic_index_in_dim(groups, mine, 1, keepdims=False)


def widen(rows):
    count = lax.axis_size("mp")
    me = lax.axis_index("mp")
    share, width = rows.shape
    bit = count // 2
    held = rows[None]
    while bit:
        taken = lax.ppermute(held, "mp", xor_pairs(count, bit))
        first = (me // bit) % 2 == 0
        held = jnp.stack(
            [jnp.where(first, held, taken), jnp.where(first, taken, held)], axis=1
        ).reshape(-1, share, width)
        bit //= 2
    return held.reshape(count * share, width)


def swap(value, axis, bit):
    return lax.ppermute(value, axis, xor_pairs(lax.axis_size(axis), bit))


def rows_of_all(rows):
    half = rows.shape[0] // 2
    across, along = swap(rows, "dp", 1), swap(rows, "mp", 2)
    first, second = swap(across[:half], "mp", 2), swap(along[half:], "dp", 1)
    mine = jnp.concatenate([rows, along, across, first, second], axis=0)
    return mine, swap(mine, "mp", 1)


def place_rows(x_ref, mine_ref, theirs_ref):
    share = mine_ref.shape[0] // 4
    here, me = lax.axis_index("dp"), lax.axis_index("mp")
    for core, ref in enumerate((mine_ref, theirs_ref)):
        for part in range(2):
            for chip in range(2):
                m = lax.rem(me // 2 + chip, 2) * 2 + lax.rem(me + core, 2)
                first = (lax.rem(here + part, 2) * 4 + m) * share
                held = (2 * part + chip) * share
                x_ref[pl.ds(pl.multiple_of(first, share), share), :] = ref[held : held + share, :]


def sum_over_all(sent, kept):
    taken = swap(sent, "mp", 1)
    total = kept + taken.astype(jnp.float32)
    here, chip = lax.axis_index("dp"), lax.axis_index("mp") // 2

    def share(part, other):
        held = lax.dynamic_index_in_dim(total, part, 0, keepdims=False)
        return lax.dynamic_index_in_dim(held, other, 0, keepdims=False)

    far = share(1 - here, 1 - chip).astype(jnp.bfloat16)
    half = far.shape[0] // 2
    for_along, for_across = swap(far[:half], "dp", 1), swap(far[half:], "mp", 2)
    along, across = share(here, 1 - chip), share(1 - here, chip)
    along = jnp.concatenate([along[:half] + for_along.astype(jnp.float32), along[half:]], axis=0)
    across = jnp.concatenate(
        [across[:half], across[half:] + for_across.astype(jnp.float32)], axis=0
    )
    return (
        share(here, chip),
        swap(across.astype(jnp.bfloat16), "dp", 1),
        swap(along.astype(jnp.bfloat16), "mp", 2),
    )


def kernel_call(kernel, outs, args, scratch=(), scalars=0):
    return pl.pallas_call(
        kernel,
        out_shape=outs,
        in_specs=[pl.BlockSpec(memory_space=pltpu.SMEM)] * scalars
        + [pl.BlockSpec(memory_space=pltpu.VMEM)] * (len(args) - scalars),
        out_specs=jax.tree.map(lambda _: pl.BlockSpec(memory_space=pltpu.VMEM), outs),
        scratch_shapes=scratch,
        compiler_params=pltpu.CompilerParams(vmem_limit_bytes=56 * 1024 * 1024),
    )(*args)


def attend(q, key_blocks, value_blocks):
    scores = [
        lax.dot_general(
            q, keys, (((1,), (1,)), ((), ())), preferred_element_type=jnp.float32
        )
        for keys in key_blocks
    ]
    top = functools.reduce(jnp.maximum, [jnp.max(s, axis=1, keepdims=True) for s in scores])
    factor = math.log2(math.e) / math.sqrt(HEAD_DIM)
    weights = [jnp.exp2((s - top) * factor) for s in scores]
    total = sum(jnp.sum(w, axis=1, keepdims=True) for w in weights)
    mixed = sum(dot(w.astype(jnp.bfloat16), v) for w, v in zip(weights, value_blocks))
    return mixed / total


def attention_kernel(count, q_ref, *refs):
    k_refs, v_refs, o_ref = refs[:count], refs[count : 2 * count], refs[2 * count]
    rows, width = q_ref.shape
    block = 128 if rows % 128 == 0 else rows

    @pl.loop(0, rows // block)
    def _(r):
        here = pl.ds(pl.multiple_of(r * block, block), block)
        for first in range(0, width, HEAD_DIM):
            columns = slice(first, first + HEAD_DIM)
            o_ref[here, columns] = attend(
                q_ref[here, columns],
                [k_ref[:, columns] for k_ref in k_refs],
                [v_ref[:, columns] for v_ref in v_refs],
            ).astype(o_ref.dtype)


def gathered_pieces(array):
    pieces = [array]
    for _ in range(lax.axis_size("seq") - 1):
        pieces.append(lax.ppermute(pieces[-1], "seq", ring_pairs("seq")))
    return pieces


def attention(queries, keys, values):
    key_pieces, value_pieces = gathered_pieces(keys), gathered_pieces(values)
    return kernel_call(
        functools.partial(attention_kernel, len(key_pieces)),
        jax.ShapeDtypeStruct(queries.shape, jnp.bfloat16),
        (queries, *key_pieces, *value_pieces),
    )


def block_columns(t, width):
    count = lax.axis_size("seq")
    block = lax.rem(lax.axis_index("seq") + (count - t), count)
    return pl.ds(pl.multiple_of(block * width, width), width)


def stream_kernel(natural, factor, stream_ref, kept_ref, taken_ref, next_ref, norm_ref):
    width = stream_ref.shape[1] // lax.axis_size("seq")
    for t in range(lax.axis_size("seq")):
        held = slice(t * width, (t + 1) * width)
        old = stream_ref[:, block_columns(t, width) if natural else held].astype(jnp.float32)
        next_ref[:, held] = old + factor * (
            kept_ref[:, held] + taken_ref[:, held].astype(jnp.float32)
        )
    norm_ref[...] = layer_norm(next_ref[...]).astype(norm_ref.dtype)


def advance(stream, kept, taken, natural):
    return kernel_call(
        functools.partial(stream_kernel, natural, 1.0),
        (
            jax.ShapeDtypeStruct(kept.shape, jnp.float32),
            jax.ShapeDtypeStruct(kept.shape, jnp.bfloat16),
        ),
        (stream, kept, taken),
    )


def last_kernel(pieces, stream_ref, *refs):
    out_ref, next_ref = refs[-2:]
    count = lax.axis_size("seq")
    width = stream_ref.shape[1] // count
    each = len(refs[:-2]) // pieces
    for t in range(count):
        first = t * width
        for c in range(pieces):
            terms = refs[c * each : (c + 1) * each]
            wide = terms[0].shape[1] // count
            held = slice(t * wide, (t + 1) * wide)
            total = sum(term[:, held].astype(jnp.float32) for term in terms)
            place = slice(first, first + wide)
            next_ref[:, place] = stream_ref[:, place] + 0.5 * total
            first += wide
    next_ref[...] = layer_norm(next_ref[...])
    for t in range(count):
        out_ref[:, block_columns(t, width)] = next_ref[:, t * width : (t + 1) * width]


def finish(stream, pieces):
    return kernel_call(
        functools.partial(last_kernel, len(pieces)),
        jax.ShapeDtypeStruct(stream.shape, jnp.float32),
        (stream, *[term for terms in pieces for term in terms]),
        [pltpu.VMEM(stream.shape, jnp.float32)],
    )


def part_columns(base, parts):
    rows, count = parts[0].shape[0], len(parts)
    if count == 1:
        return [slice(base, base + rows)]
    here = lax.axis_index("dp")
    return [
        pl.ds(pl.multiple_of(base + lax.rem(here + (count - p), count) * rows, rows), rows)
        for p in range(count)
    ]


def share_out(product_ref, sent_ref, kept_ref, columns):
    lead, share = sent_ref.shape[:-2], sent_ref.shape[-2]
    mine = lax.axis_index("mp") % 2
    for j in range(math.prod(lead)):
        theirs = pl.ds(pl.multiple_of((2 * j + 1 - mine) * share, share), share)
        ours = pl.ds(pl.multiple_of((2 * j + mine) * share, share), share)
        place = (j,) if len(lead) == 1 else (j // lead[1], j % lead[1])
        sent_ref[(*place, slice(None), columns)] = product_ref[theirs, :].astype(sent_ref.dtype)
        kept_ref[(*place, slice(None), columns)] = product_ref[ours, :]


def met(x_ref, base, parts, columns):
    return [
        dot(x_ref[:, held], part[columns]) for held, part in zip(part_columns(base, parts), parts)
    ]


def project_refs(left, weights, sent_ref, kept_ref, product_ref):
    width = product_ref.shape[1]
    for t in range(len(weights[0])):
        terms, base = [], 0
        for weight in weights:
            terms.extend(met(left, base, weight[t], slice(None)))
            base += sum(part.shape[0] for part in weight[t])
        product_ref[...] = sum(terms)
        share_out(product_ref, sent_ref, kept_ref, slice(t * width, (t + 1) * width))


def project_kernel(spec, left_ref, *refs):
    project_refs(left_ref, unpacked(spec, refs[:-3]), *refs[-3:])


def shares(rows, columns):
    count = lax.axis_size("mp")
    shape = (count // 2, rows // count, columns)
    return (
        jax.ShapeDtypeStruct(shape, jnp.bfloat16),
        jax.ShapeDtypeStruct(shape, jnp.float32),
    )


def project(left, weights):
    rows, width, number = left.shape[0], weights[0][0][0].shape[1], len(weights[0])
    arrays, spec = packed(weights)
    return kernel_call(
        functools.partial(project_kernel, spec),
        shares(rows, width * number),
        (left, *arrays),
        [pltpu.VMEM((rows, width), jnp.float32)],
    )


def heads_kernel(spec, piece_count, *refs):
    pieces, (sent_ref, kept_ref, left_ref, product_ref) = refs[:piece_count], refs[-4:]
    width = pieces[0].shape[1]
    for d, piece in enumerate(pieces):
        head = lax.rem(lax.axis_index("seq") + d, piece_count)
        left_ref[:, pl.ds(pl.multiple_of(head * width, width), width)] = piece[...]
    project_refs(left_ref, unpacked(spec, refs[piece_count:-4]), sent_ref, kept_ref, product_ref)


def project_heads(pieces, weights):
    rows, width, number = pieces[0].shape[0], weights[0][0][0].shape[1], len(weights[0])
    arrays, spec = packed(weights)
    return kernel_call(
        functools.partial(heads_kernel, spec, len(pieces)),
        shares(rows, width * number),
        (*pieces, *arrays),
        [
            pltpu.VMEM((rows, pieces[0].shape[1] * len(pieces)), jnp.bfloat16),
            pltpu.VMEM((rows, width), jnp.float32),
        ],
    )


def pack_kernel(q_ref, k_ref, v_ref, *out_refs):
    count = len(out_refs)
    width = q_ref.shape[1] // count
    for d, out_ref in enumerate(out_refs):
        head = lax.rem(lax.axis_index("seq") + d, count)
        columns = pl.ds(pl.multiple_of(head * width, width), width)
        for i, ref in enumerate((q_ref, k_ref, v_ref)):
            out_ref[:, i * width : (i + 1) * width] = ref[:, columns]


def heads_by_device(queries, keys, values):
    count = lax.axis_size("seq")
    rows, columns = queries.shape
    pieces = kernel_call(
        pack_kernel,
        [jax.ShapeDtypeStruct((rows, 3 * columns // count), queries.dtype)] * count,
        (queries, keys, values),
    )
    return [pieces[0]] + [
        lax.ppermute(pieces[d], "seq", [(i, (i + d) % count) for i in range(count)])
        for d in range(1, count)
    ]


def heads_kernel_of_all(*refs):
    count = len(refs) // 2
    width = refs[0].shape[1] // 3
    rows = refs[0].shape[0]
    block = 128 if rows % 128 == 0 else rows
    for first in range(0, width, HEAD_DIM):
        columns = [slice(i * width + first, i * width + first + HEAD_DIM) for i in range(3)]
        for in_ref, o_ref in zip(refs[:count], refs[count:]):

            @pl.loop(0, rows // block)
            def _(r):
                here = pl.ds(pl.multiple_of(r * block, block), block)
                o_ref[here, first : first + HEAD_DIM] = attend(
                    in_ref[here, columns[0]],
                    [ref[:, columns[1]] for ref in refs[:count]],
                    [ref[:, columns[2]] for ref in refs[:count]],
                ).astype(o_ref.dtype)


def attention_by_head(pieces):
    rows, columns = pieces[0].shape
    return kernel_call(
        heads_kernel_of_all,
        [jax.ShapeDtypeStruct((rows, columns // 3), jnp.bfloat16)] * len(pieces),
        tuple(pieces),
    )


def through(x_ref, weight, columns):
    width = sum(part.shape[0] for part in weight[0])
    return sum(
        term for t, parts in enumerate(weight) for term in met(x_ref, t * width, parts, columns)
    )


def column_tiles(width):
    tile = 256 if width % 256 == 0 else width
    return width // tile, tile


def gated_kernel(spec, x_ref, *refs):
    value, gate_weight = unpacked(spec, refs[:-1])
    o_ref = refs[-1]
    tiles, tile = column_tiles(o_ref.shape[1])

    @pl.loop(0, tiles)
    def _(n):
        columns = pl.ds(pl.multiple_of(n * tile, tile), tile)
        gate = through(x_ref, gate_weight, columns)
        o_ref[:, columns] = (
            through(x_ref, value, columns) / (1.0 + jnp.exp(-gate))
        ).astype(o_ref.dtype)


def gated(normed, value, gate):
    arrays, spec = packed([value, gate])
    return kernel_call(
        functools.partial(gated_kernel, spec),
        jax.ShapeDtypeStruct((normed.shape[0], value[0][0].shape[1]), jnp.bfloat16),
        (normed, *arrays),
    )


def project_all(left, weight):
    rows, width = left.shape[0], weight[0][0].shape[1]
    parts, count = lax.axis_size("dp"), lax.axis_size("mp")
    shape = (parts, count // 2, rows // (parts * count), width * len(weight))
    arrays, spec = packed([weight])
    return kernel_call(
        functools.partial(project_kernel, spec),
        (jax.ShapeDtypeStruct(shape, jnp.bfloat16), jax.ShapeDtypeStruct(shape, jnp.float32)),
        (left, *arrays),
        [pltpu.VMEM((rows, width), jnp.float32)],
    )


def conv_kernel(spec, x_ref, before_ref, after_ref, taps_ref, *refs):
    weight = unpacked(spec, refs[:-5])
    sent_ref, kept_ref, product_ref, padded_ref, active_ref = refs[-5:]
    edge, rows = before_ref.shape[0], x_ref.shape[0]
    taps = taps_ref.shape[0]
    shift = edge - taps // 2
    padded_ref[:edge, :] = before_ref[...].astype(jnp.float32)
    padded_ref[edge : edge + rows, :] = x_ref[...].astype(jnp.float32)
    padded_ref[edge + rows :, :] = after_ref[...].astype(jnp.float32)
    block = 64 if rows % 64 == 0 else rows
    for first in range(0, x_ref.shape[1], 128):
        columns = slice(first, first + 128)

        @pl.loop(0, rows // block)
        def _(r):
            base = pl.multiple_of(r * block, block)
            window = padded_ref[pl.ds(base, block + 2 * edge), columns]
            total = jnp.zeros((block, window.shape[1]), jnp.float32)
            for t in range(taps):
                total += taps_ref[t : t + 1, columns] * window[t + shift : t + shift + block]
            active_ref[pl.ds(base, block), columns] = (total / (1.0 + jnp.exp(-total))).astype(
                jnp.bfloat16
            )

    project_refs(active_ref, [weight], sent_ref, kept_ref, product_ref)


def conv_branch(units, taps, blocks, before, after):
    rows, channels = units.shape
    width = blocks[0][0].shape[1]
    arrays, spec = packed(blocks)
    return kernel_call(
        functools.partial(conv_kernel, spec),
        shares(rows, width * len(blocks)),
        (units, before, after, taps, *arrays),
        [
            pltpu.VMEM((rows, width), jnp.float32),
            pltpu.VMEM((rows + 2 * before.shape[0], channels), jnp.float32),
            pltpu.VMEM((rows, channels), jnp.bfloat16),
        ],
    )


def hidden_kernel(spec, halves, mask_ref, *refs):
    weight = unpacked(spec, refs[halves:-2])
    o_ref, x_ref = refs[-2:]
    if halves == 2:
        place_rows(x_ref, refs[0], refs[1])
    else:
        x_ref[...] = refs[0][...]
    rows, width = o_ref.shape
    tile_rows, block = rows // mask_ref.shape[0], width // mask_ref.shape[1]
    tiles, tile = column_tiles(width)

    @pl.loop(0, tiles)
    def _(n):
        units = through(x_ref, weight, pl.ds(pl.multiple_of(n * tile, tile), tile))
        units = units / (1.0 + jnp.exp(-units))
        for r in range(mask_ref.shape[0]):
            for j in range(tile // block):
                masked = (
                    units[r * tile_rows : (r + 1) * tile_rows, j * block : (j + 1) * block]
                    * mask_ref[r, n * (tile // block) + j]
                )
                o_ref[
                    r * tile_rows : (r + 1) * tile_rows,
                    pl.ds(pl.multiple_of(n * tile + j * block, block), block),
                ] = masked.astype(o_ref.dtype)


def hidden_of(rows, weight, mask):
    count = sum(piece.shape[0] for piece in rows)
    arrays, spec = packed(weight)
    return kernel_call(
        functools.partial(hidden_kernel, spec, len(rows)),
        jax.ShapeDtypeStruct((count, arrays[0].shape[1]), jnp.bfloat16),
        (mask, *rows, *arrays),
        [pltpu.VMEM((count, rows[0].shape[1]), jnp.bfloat16)],
        scalars=1,
    )


def on_device(
    residual_in,
    queries,
    keys,
    values,
    w_out,
    conv_value,
    conv_gate,
    depth_kernel,
    conv_out,
    ffn_in,
    ffn_down,
    ffn_mask,
):
    row_count = queries.shape[0]
    count, parts, here = lax.axis_size("seq"), lax.axis_size("dp"), lax.axis_index("dp")
    own_units = ffn_in.shape[1] // parts
    in_columns = lax.dynamic_slice_in_dim(ffn_in, here * own_units, own_units, axis=1)
    down_rows = lax.dynamic_slice_in_dim(ffn_down, here * own_units, own_units, axis=0)
    paired = parts == 2 and lax.axis_size("mp") == 4
    line = Line(3, 1)
    line.add(0, 4, ("w_out", w_out))
    line.add(1, 7, ("value", conv_value), ("gate", conv_gate))
    line.add(3, 8, ("conv_out", conv_out))
    by_head = queries.shape[1] % (count * HEAD_DIM) == 0
    if by_head:
        pieces = heads_by_device(queries, keys, values)
    line.begin()

    share_count = row_count // lax.axis_size("mp")
    stream = lax.dynamic_slice_in_dim(
        residual_in, lax.axis_index("mp") * share_count, share_count, 0
    )
    if by_head:
        pieces, stream = line.visits(2, (pieces, stream))
        weight_in = Gathered(pieces[0], in_columns)
        pieces = attention_by_head(pieces)
        pieces = [pieces[0]] + [
            lax.ppermute(pieces[d], "seq", [(i, (i - d) % count) for i in range(count)])
            for d in range(1, count)
        ]
        pieces = line.visits(1, pieces)
        pieces = line.until(["w_out"], pieces)
        sent, kept = project_heads(pieces, [line.take("w_out")])
    else:
        heads_out = attention(queries, keys, values)
        weight_in = Gathered(heads_out, in_columns)
        heads_out = line.until(["w_out"], heads_out)
        sent, kept = project(heads_out, [line.take("w_out")])
    cut = ffn_down.shape[1] // 2
    downs = [Gathered(kept, down_rows[:, c * cut : (c + 1) * cut]) for c in range(2)]
    kept, taken = fenced(scatter_sum, sent, kept)
    kept, taken = line.visits(2, (kept, taken))
    stream, norm_one = advance(stream, kept, taken, True)
    norm_one = fenced(widen, norm_one)
    norm_one = line.visits(1, norm_one)

    norm_one = line.until(["value", "gate"], norm_one)
    units = gated(norm_one, line.take("value"), line.take("gate"))
    edge = -(-(depth_kernel.shape[0] // 2) // 16) * 16
    up = [(i, i + 1) for i in range(count - 1)]
    before = lax.ppermute(units[row_count - edge :], "seq", up)
    after = lax.ppermute(units[:edge], "seq", [(j, i) for i, j in up])
    units = line.visits(1, units)
    units = line.until(["conv_out"], units)
    sent, kept = conv_branch(units, depth_kernel, line.take("conv_out"), before, after)
    kept, taken = fenced(scatter_sum, sent, kept)
    stream, norm_two = advance(stream, kept, taken, False)

    blocks = ffn_mask.shape[1] // parts
    mask = ffn_mask.astype(jnp.float32)
    if paired:
        rows = rows_of_all(norm_two)
        other = swap(mask, "dp", 1)
        mask = jnp.concatenate(
            [jnp.where(here == 0, mask, other), jnp.where(here == 0, other, mask)], axis=0
        )
    else:
        rows = (lax.all_gather(norm_two, ("dp", "mp"), axis=0, tiled=True),)
        mask = lax.all_gather(mask, "dp", axis=0, tiled=True)
    mask = lax.dynamic_slice_in_dim(mask, here * blocks, blocks, axis=1)
    hidden = hidden_of(rows, weight_in.take(), mask)
    pieces = []
    for down in downs:
        hidden = down.end(hidden)
        sent, kept = project_all(hidden, down.take())
        if paired:
            pieces.append(sum_over_all(sent, kept))
        else:
            mine = lax.axis_index("mp") % 2
            both = [sent.astype(jnp.float32), kept]
            both = jnp.where(mine == 0, jnp.stack(both[::-1], 2), jnp.stack(both, 2))
            pieces.append(
                (
                    lax.psum_scatter(
                        both.reshape(-1, both.shape[-1]).astype(jnp.bfloat16),
                        ("dp", "mp"),
                        scatter_dimension=0,
                        tiled=True,
                    ),
                )
            )
    return finish(stream, pieces)


def solution(mesh):
    in_specs = (
        P(("dp", "seq"), None),
        P(("dp", "seq"), "mp"),
        P(("dp", "seq"), "mp"),
        P(("dp", "seq"), "mp"),
        P("mp", "seq"),
        P("seq", "mp"),
        P("seq", "mp"),
        P(None, "mp"),
        P("mp", "seq"),
        P("seq", "mp"),
        P("mp", "seq"),
        P(("dp", "seq"), "mp"),
    )
    out_specs = P(("dp", "seq", "mp"), None)
    return jax.shard_map(
        on_device, mesh=mesh, in_specs=in_specs, out_specs=out_specs, check_vma=False
    )
```

```python
import functools
import math

import jax
import jax.numpy as jnp
from jax import lax
from jax.experimental import pallas as pl
from jax.experimental.pallas import tpu as pltpu
from jax.sharding import PartitionSpec as P

HEAD_DIM = 128


norm_epsilon = 1e-05


def ring_pairs(axis):
    count = lax.axis_size(axis)
    return [(i, (i + 1) % count) for i in range(count)]


class Rows:
    def __init__(self, array, first, count, block=None):
        self.array, self.first, self.count, self.block = array, first, count, block
        self.shape = (count, array.shape[1])

    def __getitem__(self, columns):
        if self.block is None:
            return self.array[self.first : self.first + self.count, columns]
        t, rows = self.block
        size = lax.axis_size("seq")
        start = lax.rem(lax.axis_index("seq") + (size - t), size) * rows + self.first
        return self.array[pl.ds(pl.multiple_of(start, math.gcd(rows, self.first)), self.count), columns]


class Line:
    def __init__(self, depth, lag):
        self.depth, self.lag = depth, lag
        self.waiting, self.under_way, self.crossing = [], [], []
        self.parts, self.pieces, self.needed, self.token = {}, {}, {}, None

    def add(self, first, last, *stream, shared=True):
        by_width = {}
        for name, array in stream:
            self.parts[name, 0] = [Rows(array, 0, array.shape[0])]
            self.needed[name] = lax.axis_size("dp") if shared else 1
            by_width.setdefault(array.shape[1], []).append((name, array))
        count, here = lax.axis_size("dp") if shared else 1, lax.axis_index("dp") if shared else 0
        steps = lax.axis_size("seq") - 1
        for held in by_width.values():
            fields = tuple((name, array.shape[0] // count) for name, array in held)
            own = [
                lax.dynamic_slice_in_dim(array, here * rows, rows, axis=0)
                for (_, array), (_, rows) in zip(held, fields)
            ]
            self.pieces[fields, 0] = own[0] if len(own) == 1 else jnp.concatenate(own, axis=0)
            for t in range(1, steps + 1):
                place = first + (last - first) * (t - 1) / max(steps - 1, 1)
                self.waiting.append((place, fields, t))

    def begin(self):
        self.waiting.sort(key=lambda step: step[0])
        self.refill()

    def refill(self):
        while self.waiting and len(self.under_way) < self.depth:
            _, fields, t = self.waiting[0]
            if (fields, t - 1) not in self.pieces:
                return
            del self.waiting[0]
            piece = self.pieces[fields, t - 1]
            if self.token is not None:
                piece, _ = lax.optimization_barrier((piece, self.token))
            self.under_way.append((fields, t, lax.ppermute(piece, "seq", ring_pairs("seq"))))

    def note(self, fields, t, piece):
        first = 0
        for name, rows in fields:
            self.parts.setdefault((name, t), []).append(Rows(piece, first, rows))
            first += rows

    def visit(self, beside):
        lag = self.lag if self.under_way else 0
        taken = self.crossing.pop(0) if len(self.crossing) > lag else None
        crossed = taken[2] if taken else None
        if self.under_way:
            fields, t, piece = self.under_way.pop(0)
            beside, piece, crossed = lax.optimization_barrier((beside, piece, crossed))
            self.token = self.pieces[fields, t] = piece
            self.note(fields, t, piece)
            self.refill()
            for _ in range(1, self.needed[fields[0][0]]):
                piece = lax.ppermute(piece, "dp", ring_pairs("dp"))
                self.crossing.append((fields, t, piece))
        else:
            beside, crossed = lax.optimization_barrier((beside, crossed))
        if taken:
            self.note(taken[0], taken[1], crossed)
        return beside

    def cross(self, beside):
        fields, t, taken = self.crossing.pop(0)
        beside, taken = lax.optimization_barrier((beside, taken))
        self.note(fields, t, taken)
        return beside

    def visits(self, number, beside):
        for _ in range(number * (lax.axis_size("seq") - 1) // 3):
            beside = self.visit(beside)
        return beside

    def until(self, names, beside, first=0, last=None):
        last = lax.axis_size("seq") if last is None else last
        wanted = [(name, t) for name in names for t in range(max(first, 1), last)]
        while any(len(self.parts.get(key, ())) < self.needed[key[0]] for key in wanted):
            arrived = all(key in self.parts for key in wanted)
            beside = self.cross(beside) if arrived else self.visit(beside)
        return beside

    def take(self, name, first=0, last=None):
        last = lax.axis_size("seq") if last is None else last
        here, count = lax.axis_index("dp"), lax.axis_size("dp")
        blocks = []
        for t in range(first, last):
            parts = self.parts[name, t]
            if len(parts) > 1 and parts[0].shape[0] % 128:
                held = jnp.stack([part[:] for part in parts])
                whole = jnp.concatenate(
                    [
                        lax.dynamic_index_in_dim(held, (here - q) % count, 0, keepdims=False)
                        for q in range(count)
                    ],
                    axis=0,
                )
                parts = [Rows(whole, 0, whole.shape[0])]
            blocks.append(parts)
        return blocks


class Gathered:
    def __init__(self, token, array, shared=False):
        self.rows, axes, self.other = array.shape[0], "seq", None
        self.cut = shared == "cross" and self.rows % (128 * lax.axis_size("dp")) == 0
        if shared:
            rows = self.rows // lax.axis_size("dp")
            axes = "seq" if self.cut else ("seq", "dp")
            array = lax.dynamic_slice_in_dim(array, lax.axis_index("dp") * rows, rows, axis=0)
        if token is not None:
            array, _ = lax.optimization_barrier((array, token))
        self.array = lax.all_gather(array, axes, axis=0, tiled=True)

    def cross(self, beside):
        if self.cut:
            beside, self.array = lax.optimization_barrier((beside, self.array))
            self.other = [self.array]
            for _ in range(1, lax.axis_size("dp")):
                self.other.append(lax.ppermute(self.other[-1], "dp", ring_pairs("dp")))
        return beside

    def end(self, beside):
        if self.cut:
            beside, self.other = lax.optimization_barrier((beside, self.other))
        else:
            beside, self.array = lax.optimization_barrier((beside, self.array))
        return beside

    def take(self):
        if self.cut:
            rows = self.rows // len(self.other)
            return [
                [Rows(part, 0, rows, (t, rows)) for part in self.other]
                for t in range(lax.axis_size("seq"))
            ]
        return [
            [Rows(self.array, 0, self.rows, (t, self.rows))] for t in range(lax.axis_size("seq"))
        ]


def packed(weights):
    arrays, places = [], {}

    def place(item):
        if isinstance(item, list):
            return [place(inner) for inner in item]
        if id(item.array) not in places:
            places[id(item.array)] = len(arrays)
            arrays.append(item.array)
        return places[id(item.array)], item.first, item.count, item.block

    spec = place(weights)
    return arrays, spec


def unpacked(spec, refs):
    if isinstance(spec, list):
        return [unpacked(inner, refs) for inner in spec]
    return Rows(refs[spec[0]], *spec[1:])


def layer_norm(stream):
    row_mean = jnp.mean(stream, axis=-1, keepdims=True)
    centered = stream - row_mean
    spread_of = jnp.mean(centered * centered, axis=-1, keepdims=True)
    return centered * lax.rsqrt(spread_of + norm_epsilon)


def dot(left, right):
    return jnp.dot(left, right, preferred_element_type=jnp.float32)


def xor_pairs(count, bit):
    return [(i, i ^ bit) for i in range(count)]


def fenced(function, *values):
    outs = jax.eval_shape(function, *values)
    return lax.cond(
        lax.axis_index("seq") < lax.axis_size("seq"),
        function,
        lambda *_: jax.tree.map(lambda out: jnp.zeros(out.shape, out.dtype), outs),
        *values,
    )


def scatter_sum(sent, kept):
    count = lax.axis_size("mp")
    me = lax.axis_index("mp")
    bit = 1
    while True:
        taken = lax.ppermute(sent, "mp", xor_pairs(count, bit))
        bit *= 2
        if bit == count:
            return kept[0], taken[0]
        part = kept + taken.astype(jnp.float32)
        groups = part.reshape(-1, 2, *part.shape[1:])
        mine = (me // bit) % 2
        sent = lax.dynamic_index_in_dim(groups, 1 - mine, 1, keepdims=False).astype(jnp.bfloat16)
        kept = lax.dynamic_index_in_dim(groups, mine, 1, keepdims=False)


def widen(rows):
    count = lax.axis_size("mp")
    me = lax.axis_index("mp")
    share, width = rows.shape
    bit = count // 2
    held = rows[None]
    while bit:
        taken = lax.ppermute(held, "mp", xor_pairs(count, bit))
        first = (me // bit) % 2 == 0
        held = jnp.stack(
            [jnp.where(first, held, taken), jnp.where(first, taken, held)], axis=1
        ).reshape(-1, share, width)
        bit //= 2
    return held.reshape(count * share, width)


def swap(value, axis, bit):
    return lax.ppermute(value, axis, xor_pairs(lax.axis_size(axis), bit))


def rows_of_all(rows):
    half = rows.shape[0] // 2
    across, along = swap(rows, "dp", 1), swap(rows, "mp", 2)
    first, second = swap(across[:half], "mp", 2), swap(along[half:], "dp", 1)
    mine = jnp.concatenate([rows, along, across, first, second], axis=0)
    return mine, swap(mine, "mp", 1)


def place_rows(x_ref, mine_ref, theirs_ref):
    share = mine_ref.shape[0] // 4
    here, me = lax.axis_index("dp"), lax.axis_index("mp")
    for core, ref in enumerate((mine_ref, theirs_ref)):
        for part in range(2):
            for chip in range(2):
                m = lax.rem(me // 2 + chip, 2) * 2 + lax.rem(me + core, 2)
                first = (lax.rem(here + part, 2) * 4 + m) * share
                held = (2 * part + chip) * share
                x_ref[pl.ds(pl.multiple_of(first, share), share), :] = ref[held : held + share, :]


def sum_over_all(sent, kept):
    taken = swap(sent, "mp", 1)
    total = kept + taken.astype(jnp.float32)
    here, chip = lax.axis_index("dp"), lax.axis_index("mp") // 2

    def share(part, other):
        held = lax.dynamic_index_in_dim(total, part, 0, keepdims=False)
        return lax.dynamic_index_in_dim(held, other, 0, keepdims=False)

    far = share(1 - here, 1 - chip).astype(jnp.bfloat16)
    half = far.shape[0] // 2
    for_along, for_across = swap(far[:half], "dp", 1), swap(far[half:], "mp", 2)
    along, across = share(here, 1 - chip), share(1 - here, chip)
    along = jnp.concatenate([along[:half] + for_along.astype(jnp.float32), along[half:]], axis=0)
    across = jnp.concatenate(
        [across[:half], across[half:] + for_across.astype(jnp.float32)], axis=0
    )
    return (
        share(here, chip),
        swap(across.astype(jnp.bfloat16), "dp", 1),
        swap(along.astype(jnp.bfloat16), "mp", 2),
    )


def kernel_call(kernel, outs, args, scratch=(), scalars=0):
    return pl.pallas_call(
        kernel,
        out_shape=outs,
        in_specs=[pl.BlockSpec(memory_space=pltpu.SMEM)] * scalars
        + [pl.BlockSpec(memory_space=pltpu.VMEM)] * (len(args) - scalars),
        out_specs=jax.tree.map(lambda _: pl.BlockSpec(memory_space=pltpu.VMEM), outs),
        scratch_shapes=scratch,
        compiler_params=pltpu.CompilerParams(vmem_limit_bytes=56 * 1024 * 1024),
    )(*args)


def attend(q, key_blocks, value_blocks):
    scores = [
        lax.dot_general(
            q, keys, (((1,), (1,)), ((), ())), preferred_element_type=jnp.float32
        )
        for keys in key_blocks
    ]
    top = functools.reduce(jnp.maximum, [jnp.max(s, axis=1, keepdims=True) for s in scores])
    factor = math.log2(math.e) / math.sqrt(HEAD_DIM)
    weights = [jnp.exp2((s - top) * factor) for s in scores]
    total = sum(jnp.sum(w, axis=1, keepdims=True) for w in weights)
    mixed = sum(dot(w.astype(jnp.bfloat16), v) for w, v in zip(weights, value_blocks))
    return mixed / total


def attention_kernel(count, q_ref, *refs):
    k_refs, v_refs, o_ref = refs[:count], refs[count : 2 * count], refs[2 * count]
    rows, width = q_ref.shape
    block = 128 if rows % 128 == 0 else rows

    @pl.loop(0, rows // block)
    def _(r):
        here = pl.ds(pl.multiple_of(r * block, block), block)
        for first in range(0, width, HEAD_DIM):
            columns = slice(first, first + HEAD_DIM)
            o_ref[here, columns] = attend(
                q_ref[here, columns],
                [k_ref[:, columns] for k_ref in k_refs],
                [v_ref[:, columns] for v_ref in v_refs],
            ).astype(o_ref.dtype)


def gathered_pieces(array):
    pieces = [array]
    for _ in range(lax.axis_size("seq") - 1):
        pieces.append(lax.ppermute(pieces[-1], "seq", ring_pairs("seq")))
    return pieces


def attention(queries, keys, values):
    key_pieces, value_pieces = gathered_pieces(keys), gathered_pieces(values)
    return kernel_call(
        functools.partial(attention_kernel, len(key_pieces)),
        jax.ShapeDtypeStruct(queries.shape, jnp.bfloat16),
        (queries, *key_pieces, *value_pieces),
    )


def block_columns(t, width):
    count = lax.axis_size("seq")
    block = lax.rem(lax.axis_index("seq") + (count - t), count)
    return pl.ds(pl.multiple_of(block * width, width), width)


def stream_kernel(natural, factor, stream_ref, kept_ref, taken_ref, next_ref, norm_ref):
    width = stream_ref.shape[1] // lax.axis_size("seq")
    for t in range(lax.axis_size("seq")):
        held = slice(t * width, (t + 1) * width)
        old = stream_ref[:, block_columns(t, width) if natural else held].astype(jnp.float32)
        next_ref[:, held] = old + factor * (
            kept_ref[:, held] + taken_ref[:, held].astype(jnp.float32)
        )
    norm_ref[...] = layer_norm(next_ref[...]).astype(norm_ref.dtype)


def advance(stream, kept, taken, natural):
    return kernel_call(
        functools.partial(stream_kernel, natural, 1.0),
        (
            jax.ShapeDtypeStruct(kept.shape, jnp.float32),
            jax.ShapeDtypeStruct(kept.shape, jnp.bfloat16),
        ),
        (stream, kept, taken),
    )


def last_kernel(pieces, stream_ref, *refs):
    out_ref, next_ref = refs[-2:]
    count = lax.axis_size("seq")
    width = stream_ref.shape[1] // count
    each = len(refs[:-2]) // pieces
    for t in range(count):
        first = t * width
        for c in range(pieces):
            terms = refs[c * each : (c + 1) * each]
            wide = terms[0].shape[1] // count
            held = slice(t * wide, (t + 1) * wide)
            total = sum(term[:, held].astype(jnp.float32) for term in terms)
            place = slice(first, first + wide)
            next_ref[:, place] = stream_ref[:, place] + 0.5 * total
            first += wide
    next_ref[...] = layer_norm(next_ref[...])
    for t in range(count):
        out_ref[:, block_columns(t, width)] = next_ref[:, t * width : (t + 1) * width]


def finish(stream, pieces):
    return kernel_call(
        functools.partial(last_kernel, len(pieces)),
        jax.ShapeDtypeStruct(stream.shape, jnp.float32),
        (stream, *[term for terms in pieces for term in terms]),
        [pltpu.VMEM(stream.shape, jnp.float32)],
    )


def part_columns(base, parts):
    rows, count = parts[0].shape[0], len(parts)
    if count == 1:
        return [slice(base, base + rows)]
    here = lax.axis_index("dp")
    return [
        pl.ds(pl.multiple_of(base + lax.rem(here + (count - p), count) * rows, rows), rows)
        for p in range(count)
    ]


def share_out(product_ref, sent_ref, kept_ref, columns):
    lead, share = sent_ref.shape[:-2], sent_ref.shape[-2]
    mine = lax.axis_index("mp") % 2
    for j in range(math.prod(lead)):
        theirs = pl.ds(pl.multiple_of((2 * j + 1 - mine) * share, share), share)
        ours = pl.ds(pl.multiple_of((2 * j + mine) * share, share), share)
        place = (j,) if len(lead) == 1 else (j // lead[1], j % lead[1])
        sent_ref[(*place, slice(None), columns)] = product_ref[theirs, :].astype(sent_ref.dtype)
        kept_ref[(*place, slice(None), columns)] = product_ref[ours, :]


def met(x_ref, base, parts, columns):
    return [
        dot(x_ref[:, held], part[columns]) for held, part in zip(part_columns(base, parts), parts)
    ]


def project_refs(left, weights, sent_ref, kept_ref, product_ref):
    width = product_ref.shape[1]
    for t in range(len(weights[0])):
        terms, base = [], 0
        for weight in weights:
            terms.extend(met(left, base, weight[t], slice(None)))
            base += sum(part.shape[0] for part in weight[t])
        product_ref[...] = sum(terms)
        share_out(product_ref, sent_ref, kept_ref, slice(t * width, (t + 1) * width))


def project_kernel(spec, left_ref, *refs):
    project_refs(left_ref, unpacked(spec, refs[:-3]), *refs[-3:])


def shares(rows, columns):
    count = lax.axis_size("mp")
    shape = (count // 2, rows // count, columns)
    return (
        jax.ShapeDtypeStruct(shape, jnp.bfloat16),
        jax.ShapeDtypeStruct(shape, jnp.float32),
    )


def project(left, weights):
    rows, width, number = left.shape[0], weights[0][0][0].shape[1], len(weights[0])
    arrays, spec = packed(weights)
    return kernel_call(
        functools.partial(project_kernel, spec),
        shares(rows, width * number),
        (left, *arrays),
        [pltpu.VMEM((rows, width), jnp.float32)],
    )


def heads_kernel(spec, piece_count, *refs):
    pieces, (sent_ref, kept_ref, left_ref, product_ref) = refs[:piece_count], refs[-4:]
    width = pieces[0].shape[1]
    for d, piece in enumerate(pieces):
        head = lax.rem(lax.axis_index("seq") + d, piece_count)
        left_ref[:, pl.ds(pl.multiple_of(head * width, width), width)] = piece[...]
    project_refs(left_ref, unpacked(spec, refs[piece_count:-4]), sent_ref, kept_ref, product_ref)


def project_heads(pieces, weights):
    rows, width, number = pieces[0].shape[0], weights[0][0][0].shape[1], len(weights[0])
    arrays, spec = packed(weights)
    return kernel_call(
        functools.partial(heads_kernel, spec, len(pieces)),
        shares(rows, width * number),
        (*pieces, *arrays),
        [
            pltpu.VMEM((rows, pieces[0].shape[1] * len(pieces)), jnp.bfloat16),
            pltpu.VMEM((rows, width), jnp.float32),
        ],
    )


def pack_kernel(q_ref, k_ref, v_ref, *out_refs):
    count = len(out_refs)
    width = q_ref.shape[1] // count
    for d, out_ref in enumerate(out_refs):
        head = lax.rem(lax.axis_index("seq") + d, count)
        columns = pl.ds(pl.multiple_of(head * width, width), width)
        for i, ref in enumerate((q_ref, k_ref, v_ref)):
            out_ref[:, i * width : (i + 1) * width] = ref[:, columns]


def heads_by_device(queries, keys, values):
    count = lax.axis_size("seq")
    rows, columns = queries.shape
    pieces = kernel_call(
        pack_kernel,
        [jax.ShapeDtypeStruct((rows, 3 * columns // count), queries.dtype)] * count,
        (queries, keys, values),
    )
    return [pieces[0]] + [
        lax.ppermute(pieces[d], "seq", [(i, (i + d) % count) for i in range(count)])
        for d in range(1, count)
    ]


def heads_kernel_of_all(*refs):
    count = len(refs) // 2
    width = refs[0].shape[1] // 3
    rows = refs[0].shape[0]
    block = 128 if rows % 128 == 0 else rows
    for first in range(0, width, HEAD_DIM):
        columns = [slice(i * width + first, i * width + first + HEAD_DIM) for i in range(3)]
        for in_ref, o_ref in zip(refs[:count], refs[count:]):

            @pl.loop(0, rows // block)
            def _(r):
                here = pl.ds(pl.multiple_of(r * block, block), block)
                o_ref[here, first : first + HEAD_DIM] = attend(
                    in_ref[here, columns[0]],
                    [ref[:, columns[1]] for ref in refs[:count]],
                    [ref[:, columns[2]] for ref in refs[:count]],
                ).astype(o_ref.dtype)


def attention_by_head(pieces):
    rows, columns = pieces[0].shape
    return kernel_call(
        heads_kernel_of_all,
        [jax.ShapeDtypeStruct((rows, columns // 3), jnp.bfloat16)] * len(pieces),
        tuple(pieces),
    )


def through(x_ref, weight, columns):
    width = sum(part.shape[0] for part in weight[0])
    return sum(
        term for t, parts in enumerate(weight) for term in met(x_ref, t * width, parts, columns)
    )


def column_tiles(width):
    tile = 256 if width % 256 == 0 else width
    return width // tile, tile


def gated_kernel(spec, x_ref, *refs):
    value, gate_weight = unpacked(spec, refs[:-1])
    o_ref = refs[-1]
    tiles, tile = column_tiles(o_ref.shape[1])

    @pl.loop(0, tiles)
    def _(n):
        columns = pl.ds(pl.multiple_of(n * tile, tile), tile)
        gate = through(x_ref, gate_weight, columns)
        o_ref[:, columns] = (
            through(x_ref, value, columns) / (1.0 + jnp.exp(-gate))
        ).astype(o_ref.dtype)


def gated(normed, value, gate):
    arrays, spec = packed([value, gate])
    return kernel_call(
        functools.partial(gated_kernel, spec),
        jax.ShapeDtypeStruct((normed.shape[0], value[0][0].shape[1]), jnp.bfloat16),
        (normed, *arrays),
    )


def project_all(left, weight):
    rows, width = left.shape[0], weight[0][0].shape[1]
    parts, count = lax.axis_size("dp"), lax.axis_size("mp")
    shape = (parts, count // 2, rows // (parts * count), width * len(weight))
    arrays, spec = packed([weight])
    return kernel_call(
        functools.partial(project_kernel, spec),
        (jax.ShapeDtypeStruct(shape, jnp.bfloat16), jax.ShapeDtypeStruct(shape, jnp.float32)),
        (left, *arrays),
        [pltpu.VMEM((rows, width), jnp.float32)],
    )


def conv_kernel(spec, x_ref, before_ref, after_ref, taps_ref, *refs):
    weight = unpacked(spec, refs[:-5])
    sent_ref, kept_ref, product_ref, padded_ref, active_ref = refs[-5:]
    edge, rows = before_ref.shape[0], x_ref.shape[0]
    taps = taps_ref.shape[0]
    shift = edge - taps // 2
    padded_ref[:edge, :] = before_ref[...].astype(jnp.float32)
    padded_ref[edge : edge + rows, :] = x_ref[...].astype(jnp.float32)
    padded_ref[edge + rows :, :] = after_ref[...].astype(jnp.float32)
    block = 64 if rows % 64 == 0 else rows
    for first in range(0, x_ref.shape[1], 128):
        columns = slice(first, first + 128)

        @pl.loop(0, rows // block)
        def _(r):
            base = pl.multiple_of(r * block, block)
            window = padded_ref[pl.ds(base, block + 2 * edge), columns]
            total = jnp.zeros((block, window.shape[1]), jnp.float32)
            for t in range(taps):
                total += taps_ref[t : t + 1, columns] * window[t + shift : t + shift + block]
            active_ref[pl.ds(base, block), columns] = (total / (1.0 + jnp.exp(-total))).astype(
                jnp.bfloat16
            )

    project_refs(active_ref, [weight], sent_ref, kept_ref, product_ref)


def conv_branch(units, taps, blocks, before, after):
    rows, channels = units.shape
    width = blocks[0][0].shape[1]
    arrays, spec = packed(blocks)
    return kernel_call(
        functools.partial(conv_kernel, spec),
        shares(rows, width * len(blocks)),
        (units, before, after, taps, *arrays),
        [
            pltpu.VMEM((rows, width), jnp.float32),
            pltpu.VMEM((rows + 2 * before.shape[0], channels), jnp.float32),
            pltpu.VMEM((rows, channels), jnp.bfloat16),
        ],
    )


def hidden_kernel(spec, halves, mask_ref, *refs):
    weight = unpacked(spec, refs[halves:-2])
    o_ref, x_ref = refs[-2:]
    if halves == 2:
        place_rows(x_ref, refs[0], refs[1])
    else:
        x_ref[...] = refs[0][...]
    rows, width = o_ref.shape
    tile_rows, block = rows // mask_ref.shape[0], width // mask_ref.shape[1]
    tiles, tile = column_tiles(width)

    @pl.loop(0, tiles)
    def _(n):
        units = through(x_ref, weight, pl.ds(pl.multiple_of(n * tile, tile), tile))
        units = units / (1.0 + jnp.exp(-units))
        for r in range(mask_ref.shape[0]):
            for j in range(tile // block):
                masked = (
                    units[r * tile_rows : (r + 1) * tile_rows, j * block : (j + 1) * block]
                    * mask_ref[r, n * (tile // block) + j]
                )
                o_ref[
                    r * tile_rows : (r + 1) * tile_rows,
                    pl.ds(pl.multiple_of(n * tile + j * block, block), block),
                ] = masked.astype(o_ref.dtype)


def hidden_of(rows, weight, mask):
    count = sum(piece.shape[0] for piece in rows)
    arrays, spec = packed(weight)
    return kernel_call(
        functools.partial(hidden_kernel, spec, len(rows)),
        jax.ShapeDtypeStruct((count, arrays[0].shape[1]), jnp.bfloat16),
        (mask, *rows, *arrays),
        [pltpu.VMEM((count, rows[0].shape[1]), jnp.bfloat16)],
        scalars=1,
    )


def on_device(
    residual_in,
    queries,
    keys,
    values,
    w_out,
    conv_value,
    conv_gate,
    depth_kernel,
    conv_out,
    ffn_in,
    ffn_down,
    ffn_mask,
):
    row_count = queries.shape[0]
    count, parts, here = lax.axis_size("seq"), lax.axis_size("dp"), lax.axis_index("dp")
    own_units = ffn_in.shape[1] // parts
    in_columns = lax.dynamic_slice_in_dim(ffn_in, here * own_units, own_units, axis=1)
    down_rows = lax.dynamic_slice_in_dim(ffn_down, here * own_units, own_units, axis=0)
    paired = parts == 2 and lax.axis_size("mp") == 4
    line = Line(3, 1)
    line.add(0, 4, ("value", conv_value), ("gate", conv_gate))
    line.add(1, 5, ("conv_out", conv_out))
    by_head = queries.shape[1] % (count * HEAD_DIM) == 0
    if by_head:
        pieces = heads_by_device(queries, keys, values)
    wide = ffn_down.shape[1]
    last = 128 if wide % (2 * 128) == 0 else wide // 2
    line.add(6, 8, ("down", down_rows[:, wide - last :]), shared=False)
    line.begin()
    weight_out = Gathered(None, w_out, True)

    share_count = row_count // lax.axis_size("mp")
    stream = lax.dynamic_slice_in_dim(
        residual_in, lax.axis_index("mp") * share_count, share_count, 0
    )
    weight_in = Gathered(None, in_columns)
    if by_head:
        pieces, stream = line.visits(1, (pieces, stream))
        pieces = weight_out.cross(pieces)
        pieces = attention_by_head(pieces)
        pieces = [pieces[0]] + [
            lax.ppermute(pieces[d], "seq", [(i, (i - d) % count) for i in range(count)])
            for d in range(1, count)
        ]
        pieces = line.visits(2, pieces)
        pieces = weight_out.end(pieces)
        sent, kept = project_heads(pieces, [weight_out.take()])
    else:
        heads_out = attention(queries, keys, values)
        heads_out = weight_out.end(weight_out.cross(heads_out))
        sent, kept = project(heads_out, [weight_out.take()])
    downs = [Gathered(kept, down_rows[:, : wide - last])]
    kept, taken = fenced(scatter_sum, sent, kept)
    kept, taken = line.visits(2, (kept, taken))
    stream, norm_one = advance(stream, kept, taken, True)
    norm_one = fenced(widen, norm_one)
    norm_one = line.visits(1, norm_one)

    norm_one = line.until(["value", "gate"], norm_one)
    units = gated(norm_one, line.take("value"), line.take("gate"))
    edge = -(-(depth_kernel.shape[0] // 2) // 16) * 16
    up = [(i, i + 1) for i in range(count - 1)]
    before = lax.ppermute(units[row_count - edge :], "seq", up)
    after = lax.ppermute(units[:edge], "seq", [(j, i) for i, j in up])
    units = line.visits(0, units)
    units = line.until(["conv_out"], units)
    sent, kept = conv_branch(units, depth_kernel, line.take("conv_out"), before, after)
    kept, taken = fenced(scatter_sum, sent, kept)
    kept, taken = line.visits(2, (kept, taken))
    stream, norm_two = advance(stream, kept, taken, False)

    blocks = ffn_mask.shape[1] // parts
    mask = ffn_mask.astype(jnp.float32)
    if paired:
        rows = rows_of_all(norm_two)
        other = swap(mask, "dp", 1)
        mask = jnp.concatenate(
            [jnp.where(here == 0, mask, other), jnp.where(here == 0, other, mask)], axis=0
        )
    else:
        rows = (lax.all_gather(norm_two, ("dp", "mp"), axis=0, tiled=True),)
        mask = lax.all_gather(mask, "dp", axis=0, tiled=True)
    mask = lax.dynamic_slice_in_dim(mask, here * blocks, blocks, axis=1)
    rows = line.visits(0, rows)
    hidden = hidden_of(rows, weight_in.take(), mask)
    hidden = line.visits(0, hidden)
    pieces = []
    for down in [None, *downs]:
        if down is None:
            hidden = line.until(["down"], hidden)
            sent, kept = project_all(hidden, line.take("down"))
        else:
            if pieces and paired:
                hidden, pieces[-1] = down.end((hidden, pieces[-1]))
            else:
                hidden = down.end(hidden)
            sent, kept = project_all(hidden, down.take())
        if paired:
            pieces.append(sum_over_all(sent, kept))
        else:
            mine = lax.axis_index("mp") % 2
            both = [sent.astype(jnp.float32), kept]
            both = jnp.where(mine == 0, jnp.stack(both[::-1], 2), jnp.stack(both, 2))
            pieces.append(
                (
                    lax.psum_scatter(
                        both.reshape(-1, both.shape[-1]).astype(jnp.bfloat16),
                        ("dp", "mp"),
                        scatter_dimension=0,
                        tiled=True,
                    ),
                )
            )
    return finish(stream, [*pieces[1:], pieces[0]])


def solution(mesh):
    in_specs = (
        P(("dp", "seq"), None),
        P(("dp", "seq"), "mp"),
        P(("dp", "seq"), "mp"),
        P(("dp", "seq"), "mp"),
        P("mp", "seq"),
        P("seq", "mp"),
        P("seq", "mp"),
        P(None, "mp"),
        P("mp", "seq"),
        P("seq", "mp"),
        P("mp", "seq"),
        P(("dp", "seq"), "mp"),
    )
    out_specs = P(("dp", "seq", "mp"), None)
    return jax.shard_map(
        on_device, mesh=mesh, in_specs=in_specs, out_specs=out_specs, check_vma=False
    )
```

```python
import functools
import math

import jax
import jax.numpy as jnp
from jax import lax
from jax.experimental import pallas as pl
from jax.experimental.pallas import tpu as pltpu
from jax.sharding import PartitionSpec as P

HEAD_DIM = 128


norm_epsilon = 1e-05


def ring_pairs(axis):
    count = lax.axis_size(axis)
    return [(i, (i + 1) % count) for i in range(count)]


class Rows:
    def __init__(self, array, first, count, block=None):
        self.array, self.first, self.count, self.block = array, first, count, block
        self.shape = (count, array.shape[1])

    def __getitem__(self, columns):
        if self.block is None:
            return self.array[self.first : self.first + self.count, columns]
        t, rows = self.block
        size = lax.axis_size("seq")
        start = lax.rem(lax.axis_index("seq") + (size - t), size) * rows + self.first
        return self.array[pl.ds(pl.multiple_of(start, math.gcd(rows, self.first)), self.count), columns]


class Line:
    def __init__(self, depth, lag):
        self.depth, self.lag = depth, lag
        self.waiting, self.under_way, self.crossing = [], [], []
        self.parts, self.pieces, self.needed, self.token = {}, {}, {}, None

    def add(self, first, last, *stream, shared=True):
        by_width = {}
        for name, array in stream:
            self.parts[name, 0] = [Rows(array, 0, array.shape[0])]
            self.needed[name] = lax.axis_size("dp") if shared else 1
            by_width.setdefault(array.shape[1], []).append((name, array))
        count, here = lax.axis_size("dp") if shared else 1, lax.axis_index("dp") if shared else 0
        steps = lax.axis_size("seq") - 1
        for held in by_width.values():
            fields = tuple((name, array.shape[0] // count) for name, array in held)
            own = [
                lax.dynamic_slice_in_dim(array, here * rows, rows, axis=0)
                for (_, array), (_, rows) in zip(held, fields)
            ]
            self.pieces[fields, 0] = own[0] if len(own) == 1 else jnp.concatenate(own, axis=0)
            for t in range(1, steps + 1):
                place = first + (last - first) * (t - 1) / max(steps - 1, 1)
                self.waiting.append((place, fields, t))

    def begin(self):
        self.waiting.sort(key=lambda step: step[0])
        self.refill()

    def refill(self):
        while self.waiting and len(self.under_way) < self.depth:
            _, fields, t = self.waiting[0]
            if (fields, t - 1) not in self.pieces:
                return
            del self.waiting[0]
            piece = self.pieces[fields, t - 1]
            if self.token is not None:
                piece, _ = lax.optimization_barrier((piece, self.token))
            self.under_way.append((fields, t, lax.ppermute(piece, "seq", ring_pairs("seq"))))

    def note(self, fields, t, piece):
        first = 0
        for name, rows in fields:
            self.parts.setdefault((name, t), []).append(Rows(piece, first, rows))
            first += rows

    def visit(self, beside):
        lag = self.lag if self.under_way else 0
        taken = self.crossing.pop(0) if len(self.crossing) > lag else None
        crossed = taken[2] if taken else None
        if self.under_way:
            fields, t, piece = self.under_way.pop(0)
            beside, piece, crossed = lax.optimization_barrier((beside, piece, crossed))
            self.token = self.pieces[fields, t] = piece
            self.note(fields, t, piece)
            self.refill()
            for _ in range(1, self.needed[fields[0][0]]):
                piece = lax.ppermute(piece, "dp", ring_pairs("dp"))
                self.crossing.append((fields, t, piece))
        else:
            beside, crossed = lax.optimization_barrier((beside, crossed))
        if taken:
            self.note(taken[0], taken[1], crossed)
        return beside

    def cross(self, beside):
        fields, t, taken = self.crossing.pop(0)
        beside, taken = lax.optimization_barrier((beside, taken))
        self.note(fields, t, taken)
        return beside

    def visits(self, number, beside):
        for _ in range(number * (lax.axis_size("seq") - 1) // 3):
            beside = self.visit(beside)
        return beside

    def until(self, names, beside, first=0, last=None):
        last = lax.axis_size("seq") if last is None else last
        wanted = [(name, t) for name in names for t in range(max(first, 1), last)]
        while any(len(self.parts.get(key, ())) < self.needed[key[0]] for key in wanted):
            arrived = all(key in self.parts for key in wanted)
            beside = self.cross(beside) if arrived else self.visit(beside)
        return beside

    def take(self, name, first=0, last=None):
        last = lax.axis_size("seq") if last is None else last
        here, count = lax.axis_index("dp"), lax.axis_size("dp")
        blocks = []
        for t in range(first, last):
            parts = self.parts[name, t]
            if len(parts) > 1 and parts[0].shape[0] % 128:
                held = jnp.stack([part[:] for part in parts])
                whole = jnp.concatenate(
                    [
                        lax.dynamic_index_in_dim(held, (here - q) % count, 0, keepdims=False)
                        for q in range(count)
                    ],
                    axis=0,
                )
                parts = [Rows(whole, 0, whole.shape[0])]
            blocks.append(parts)
        return blocks


class Gathered:
    def __init__(self, token, array, shared=False):
        self.rows, axes, self.other = array.shape[0], "seq", None
        self.cut = shared == "cross" and self.rows % (128 * lax.axis_size("dp")) == 0
        if shared:
            rows = self.rows // lax.axis_size("dp")
            axes = "seq" if self.cut else ("seq", "dp")
            array = lax.dynamic_slice_in_dim(array, lax.axis_index("dp") * rows, rows, axis=0)
        if token is not None:
            array, _ = lax.optimization_barrier((array, token))
        self.array = lax.all_gather(array, axes, axis=0, tiled=True)

    def cross(self, beside):
        if self.cut:
            beside, self.array = lax.optimization_barrier((beside, self.array))
            self.other = [self.array]
            for _ in range(1, lax.axis_size("dp")):
                self.other.append(lax.ppermute(self.other[-1], "dp", ring_pairs("dp")))
        return beside

    def end(self, beside):
        if self.cut:
            beside, self.other = lax.optimization_barrier((beside, self.other))
        else:
            beside, self.array = lax.optimization_barrier((beside, self.array))
        return beside

    def take(self):
        if self.cut:
            rows = self.rows // len(self.other)
            return [
                [Rows(part, 0, rows, (t, rows)) for part in self.other]
                for t in range(lax.axis_size("seq"))
            ]
        return [
            [Rows(self.array, 0, self.rows, (t, self.rows))] for t in range(lax.axis_size("seq"))
        ]


def packed(weights):
    arrays, places = [], {}

    def place(item):
        if isinstance(item, list):
            return [place(inner) for inner in item]
        if id(item.array) not in places:
            places[id(item.array)] = len(arrays)
            arrays.append(item.array)
        return places[id(item.array)], item.first, item.count, item.block

    spec = place(weights)
    return arrays, spec


def unpacked(spec, refs):
    if isinstance(spec, list):
        return [unpacked(inner, refs) for inner in spec]
    return Rows(refs[spec[0]], *spec[1:])


def layer_norm(stream):
    row_mean = jnp.mean(stream, axis=-1, keepdims=True)
    centered = stream - row_mean
    spread_of = jnp.mean(centered * centered, axis=-1, keepdims=True)
    return centered * lax.rsqrt(spread_of + norm_epsilon)


def dot(left, right):
    return jnp.dot(left, right, preferred_element_type=jnp.float32)


def xor_pairs(count, bit):
    return [(i, i ^ bit) for i in range(count)]


def fenced(function, *values):
    outs = jax.eval_shape(function, *values)
    return lax.cond(
        lax.axis_index("seq") < lax.axis_size("seq"),
        function,
        lambda *_: jax.tree.map(lambda out: jnp.zeros(out.shape, out.dtype), outs),
        *values,
    )


def scatter_sum(sent, kept):
    count = lax.axis_size("mp")
    me = lax.axis_index("mp")
    bit = 1
    while True:
        taken = lax.ppermute(sent, "mp", xor_pairs(count, bit))
        bit *= 2
        if bit == count:
            return kept[0], taken[0]
        part = kept + taken.astype(jnp.float32)
        groups = part.reshape(-1, 2, *part.shape[1:])
        mine = (me // bit) % 2
        sent = lax.dynamic_index_in_dim(groups, 1 - mine, 1, keepdims=False).astype(jnp.bfloat16)
        kept = lax.dynamic_index_in_dim(groups, mine, 1, keepdims=False)


def widen(rows):
    count = lax.axis_size("mp")
    me = lax.axis_index("mp")
    share, width = rows.shape
    bit = count // 2
    held = rows[None]
    while bit:
        taken = lax.ppermute(held, "mp", xor_pairs(count, bit))
        first = (me // bit) % 2 == 0
        held = jnp.stack(
            [jnp.where(first, held, taken), jnp.where(first, taken, held)], axis=1
        ).reshape(-1, share, width)
        bit //= 2
    return held.reshape(count * share, width)


def swap(value, axis, bit):
    return lax.ppermute(value, axis, xor_pairs(lax.axis_size(axis), bit))


def rows_of_all(rows):
    half = rows.shape[0] // 2
    across, along = swap(rows, "dp", 1), swap(rows, "mp", 2)
    first, second = swap(across[:half], "mp", 2), swap(along[half:], "dp", 1)
    mine = jnp.concatenate([rows, along, across, first, second], axis=0)
    return mine, swap(mine, "mp", 1)


def place_rows(x_ref, mine_ref, theirs_ref):
    share = mine_ref.shape[0] // 4
    here, me = lax.axis_index("dp"), lax.axis_index("mp")
    for core, ref in enumerate((mine_ref, theirs_ref)):
        for part in range(2):
            for chip in range(2):
                m = lax.rem(me // 2 + chip, 2) * 2 + lax.rem(me + core, 2)
                first = (lax.rem(here + part, 2) * 4 + m) * share
                held = (2 * part + chip) * share
                x_ref[pl.ds(pl.multiple_of(first, share), share), :] = ref[held : held + share, :]


def sum_over_all(sent, kept):
    taken = swap(sent, "mp", 1)
    total = kept + taken.astype(jnp.float32)
    here, chip = lax.axis_index("dp"), lax.axis_index("mp") // 2

    def share(part, other):
        held = lax.dynamic_index_in_dim(total, part, 0, keepdims=False)
        return lax.dynamic_index_in_dim(held, other, 0, keepdims=False)

    far = share(1 - here, 1 - chip).astype(jnp.bfloat16)
    half = far.shape[0] // 2
    for_along, for_across = swap(far[:half], "dp", 1), swap(far[half:], "mp", 2)
    along, across = share(here, 1 - chip), share(1 - here, chip)
    along = jnp.concatenate([along[:half] + for_along.astype(jnp.float32), along[half:]], axis=0)
    across = jnp.concatenate(
        [across[:half], across[half:] + for_across.astype(jnp.float32)], axis=0
    )
    return (
        share(here, chip),
        swap(across.astype(jnp.bfloat16), "dp", 1),
        swap(along.astype(jnp.bfloat16), "mp", 2),
    )


def kernel_call(kernel, outs, args, scratch=(), scalars=0):
    return pl.pallas_call(
        kernel,
        out_shape=outs,
        in_specs=[pl.BlockSpec(memory_space=pltpu.SMEM)] * scalars
        + [pl.BlockSpec(memory_space=pltpu.VMEM)] * (len(args) - scalars),
        out_specs=jax.tree.map(lambda _: pl.BlockSpec(memory_space=pltpu.VMEM), outs),
        scratch_shapes=scratch,
        compiler_params=pltpu.CompilerParams(vmem_limit_bytes=56 * 1024 * 1024),
    )(*args)


def attend(q, key_blocks, value_blocks):
    scores = [
        lax.dot_general(
            q, keys, (((1,), (1,)), ((), ())), preferred_element_type=jnp.float32
        )
        for keys in key_blocks
    ]
    top = functools.reduce(jnp.maximum, [jnp.max(s, axis=1, keepdims=True) for s in scores])
    factor = math.log2(math.e) / math.sqrt(HEAD_DIM)
    weights = [jnp.exp2((s - top) * factor) for s in scores]
    total = sum(jnp.sum(w, axis=1, keepdims=True) for w in weights)
    mixed = sum(dot(w.astype(jnp.bfloat16), v) for w, v in zip(weights, value_blocks))
    return mixed / total


def attention_kernel(count, q_ref, *refs):
    k_refs, v_refs, o_ref = refs[:count], refs[count : 2 * count], refs[2 * count]
    rows, width = q_ref.shape
    block = 128 if rows % 128 == 0 else rows

    @pl.loop(0, rows // block)
    def _(r):
        here = pl.ds(pl.multiple_of(r * block, block), block)
        for first in range(0, width, HEAD_DIM):
            columns = slice(first, first + HEAD_DIM)
            o_ref[here, columns] = attend(
                q_ref[here, columns],
                [k_ref[:, columns] for k_ref in k_refs],
                [v_ref[:, columns] for v_ref in v_refs],
            ).astype(o_ref.dtype)


def gathered_pieces(array):
    pieces = [array]
    for _ in range(lax.axis_size("seq") - 1):
        pieces.append(lax.ppermute(pieces[-1], "seq", ring_pairs("seq")))
    return pieces


def attention(queries, keys, values):
    key_pieces, value_pieces = gathered_pieces(keys), gathered_pieces(values)
    return kernel_call(
        functools.partial(attention_kernel, len(key_pieces)),
        jax.ShapeDtypeStruct(queries.shape, jnp.bfloat16),
        (queries, *key_pieces, *value_pieces),
    )


def block_columns(t, width):
    count = lax.axis_size("seq")
    block = lax.rem(lax.axis_index("seq") + (count - t), count)
    return pl.ds(pl.multiple_of(block * width, width), width)


def stream_kernel(natural, factor, stream_ref, kept_ref, taken_ref, next_ref, norm_ref):
    width = stream_ref.shape[1] // lax.axis_size("seq")
    for t in range(lax.axis_size("seq")):
        held = slice(t * width, (t + 1) * width)
        old = stream_ref[:, block_columns(t, width) if natural else held].astype(jnp.float32)
        next_ref[:, held] = old + factor * (
            kept_ref[:, held] + taken_ref[:, held].astype(jnp.float32)
        )
    norm_ref[...] = layer_norm(next_ref[...]).astype(norm_ref.dtype)


def advance(stream, kept, taken, natural):
    return kernel_call(
        functools.partial(stream_kernel, natural, 1.0),
        (
            jax.ShapeDtypeStruct(kept.shape, jnp.float32),
            jax.ShapeDtypeStruct(kept.shape, jnp.bfloat16),
        ),
        (stream, kept, taken),
    )


def last_kernel(pieces, stream_ref, *refs):
    out_ref, next_ref = refs[-2:]
    count = lax.axis_size("seq")
    width = stream_ref.shape[1] // count
    each = len(refs[:-2]) // pieces
    for t in range(count):
        first = t * width
        for c in range(pieces):
            terms = refs[c * each : (c + 1) * each]
            wide = terms[0].shape[1] // count
            held = slice(t * wide, (t + 1) * wide)
            total = sum(term[:, held].astype(jnp.float32) for term in terms)
            place = slice(first, first + wide)
            next_ref[:, place] = stream_ref[:, place] + 0.5 * total
            first += wide
    next_ref[...] = layer_norm(next_ref[...])
    for t in range(count):
        out_ref[:, block_columns(t, width)] = next_ref[:, t * width : (t + 1) * width]


def finish(stream, pieces):
    return kernel_call(
        functools.partial(last_kernel, len(pieces)),
        jax.ShapeDtypeStruct(stream.shape, jnp.float32),
        (stream, *[term for terms in pieces for term in terms]),
        [pltpu.VMEM(stream.shape, jnp.float32)],
    )


def part_columns(base, parts):
    rows, count = parts[0].shape[0], len(parts)
    if count == 1:
        return [slice(base, base + rows)]
    here = lax.axis_index("dp")
    return [
        pl.ds(pl.multiple_of(base + lax.rem(here + (count - p), count) * rows, rows), rows)
        for p in range(count)
    ]


def share_out(product_ref, sent_ref, kept_ref, columns):
    lead, share = sent_ref.shape[:-2], sent_ref.shape[-2]
    mine = lax.axis_index("mp") % 2
    for j in range(math.prod(lead)):
        theirs = pl.ds(pl.multiple_of((2 * j + 1 - mine) * share, share), share)
        ours = pl.ds(pl.multiple_of((2 * j + mine) * share, share), share)
        place = (j,) if len(lead) == 1 else (j // lead[1], j % lead[1])
        sent_ref[(*place, slice(None), columns)] = product_ref[theirs, :].astype(sent_ref.dtype)
        kept_ref[(*place, slice(None), columns)] = product_ref[ours, :]


def met(x_ref, base, parts, columns):
    return [
        dot(x_ref[:, held], part[columns]) for held, part in zip(part_columns(base, parts), parts)
    ]


def project_refs(left, weights, sent_ref, kept_ref, product_ref):
    width = product_ref.shape[1]
    for t in range(len(weights[0])):
        terms, base = [], 0
        for weight in weights:
            terms.extend(met(left, base, weight[t], slice(None)))
            base += sum(part.shape[0] for part in weight[t])
        product_ref[...] = sum(terms)
        share_out(product_ref, sent_ref, kept_ref, slice(t * width, (t + 1) * width))


def project_kernel(spec, left_ref, *refs):
    project_refs(left_ref, unpacked(spec, refs[:-3]), *refs[-3:])


def shares(rows, columns):
    count = lax.axis_size("mp")
    shape = (count // 2, rows // count, columns)
    return (
        jax.ShapeDtypeStruct(shape, jnp.bfloat16),
        jax.ShapeDtypeStruct(shape, jnp.float32),
    )


def project(left, weights):
    rows, width, number = left.shape[0], weights[0][0][0].shape[1], len(weights[0])
    arrays, spec = packed(weights)
    return kernel_call(
        functools.partial(project_kernel, spec),
        shares(rows, width * number),
        (left, *arrays),
        [pltpu.VMEM((rows, width), jnp.float32)],
    )


def heads_kernel(spec, piece_count, *refs):
    pieces, (sent_ref, kept_ref, left_ref, product_ref) = refs[:piece_count], refs[-4:]
    width = pieces[0].shape[1]
    for d, piece in enumerate(pieces):
        head = lax.rem(lax.axis_index("seq") + d, piece_count)
        left_ref[:, pl.ds(pl.multiple_of(head * width, width), width)] = piece[...]
    project_refs(left_ref, unpacked(spec, refs[piece_count:-4]), sent_ref, kept_ref, product_ref)


def project_heads(pieces, weights):
    rows, width, number = pieces[0].shape[0], weights[0][0][0].shape[1], len(weights[0])
    arrays, spec = packed(weights)
    return kernel_call(
        functools.partial(heads_kernel, spec, len(pieces)),
        shares(rows, width * number),
        (*pieces, *arrays),
        [
            pltpu.VMEM((rows, pieces[0].shape[1] * len(pieces)), jnp.bfloat16),
            pltpu.VMEM((rows, width), jnp.float32),
        ],
    )


def pack_kernel(q_ref, k_ref, v_ref, *out_refs):
    count = len(out_refs)
    width = q_ref.shape[1] // count
    for d, out_ref in enumerate(out_refs):
        head = lax.rem(lax.axis_index("seq") + d, count)
        columns = pl.ds(pl.multiple_of(head * width, width), width)
        for i, ref in enumerate((q_ref, k_ref, v_ref)):
            out_ref[:, i * width : (i + 1) * width] = ref[:, columns]


def heads_by_device(queries, keys, values):
    count = lax.axis_size("seq")
    rows, columns = queries.shape
    pieces = kernel_call(
        pack_kernel,
        [jax.ShapeDtypeStruct((rows, 3 * columns // count), queries.dtype)] * count,
        (queries, keys, values),
    )
    return [pieces[0]] + [
        lax.ppermute(pieces[d], "seq", [(i, (i + d) % count) for i in range(count)])
        for d in range(1, count)
    ]


def heads_kernel_of_all(*refs):
    count = len(refs) // 2
    width = refs[0].shape[1] // 3
    rows = refs[0].shape[0]
    block = 128 if rows % 128 == 0 else rows
    for first in range(0, width, HEAD_DIM):
        columns = [slice(i * width + first, i * width + first + HEAD_DIM) for i in range(3)]
        for in_ref, o_ref in zip(refs[:count], refs[count:]):

            @pl.loop(0, rows // block)
            def _(r):
                here = pl.ds(pl.multiple_of(r * block, block), block)
                o_ref[here, first : first + HEAD_DIM] = attend(
                    in_ref[here, columns[0]],
                    [ref[:, columns[1]] for ref in refs[:count]],
                    [ref[:, columns[2]] for ref in refs[:count]],
                ).astype(o_ref.dtype)


def attention_by_head(pieces):
    rows, columns = pieces[0].shape
    return kernel_call(
        heads_kernel_of_all,
        [jax.ShapeDtypeStruct((rows, columns // 3), jnp.bfloat16)] * len(pieces),
        tuple(pieces),
    )


def through(x_ref, weight, columns):
    width = sum(part.shape[0] for part in weight[0])
    return sum(
        term for t, parts in enumerate(weight) for term in met(x_ref, t * width, parts, columns)
    )


def column_tiles(width):
    tile = 256 if width % 256 == 0 else width
    return width // tile, tile


def gated_kernel(spec, x_ref, *refs):
    value, gate_weight = unpacked(spec, refs[:-1])
    o_ref = refs[-1]
    tiles, tile = column_tiles(o_ref.shape[1])

    @pl.loop(0, tiles)
    def _(n):
        columns = pl.ds(pl.multiple_of(n * tile, tile), tile)
        gate = through(x_ref, gate_weight, columns)
        o_ref[:, columns] = (
            through(x_ref, value, columns) / (1.0 + jnp.exp(-gate))
        ).astype(o_ref.dtype)


def gated(normed, value, gate):
    arrays, spec = packed([value, gate])
    return kernel_call(
        functools.partial(gated_kernel, spec),
        jax.ShapeDtypeStruct((normed.shape[0], value[0][0].shape[1]), jnp.bfloat16),
        (normed, *arrays),
    )


def project_all(left, weight):
    rows, width = left.shape[0], weight[0][0].shape[1]
    parts, count = lax.axis_size("dp"), lax.axis_size("mp")
    shape = (parts, count // 2, rows // (parts * count), width * len(weight))
    arrays, spec = packed([weight])
    return kernel_call(
        functools.partial(project_kernel, spec),
        (jax.ShapeDtypeStruct(shape, jnp.bfloat16), jax.ShapeDtypeStruct(shape, jnp.float32)),
        (left, *arrays),
        [pltpu.VMEM((rows, width), jnp.float32)],
    )


def conv_kernel(spec, x_ref, before_ref, after_ref, taps_ref, *refs):
    weight = unpacked(spec, refs[:-5])
    sent_ref, kept_ref, product_ref, padded_ref, active_ref = refs[-5:]
    edge, rows = before_ref.shape[0], x_ref.shape[0]
    taps = taps_ref.shape[0]
    shift = edge - taps // 2
    padded_ref[:edge, :] = before_ref[...].astype(jnp.float32)
    padded_ref[edge : edge + rows, :] = x_ref[...].astype(jnp.float32)
    padded_ref[edge + rows :, :] = after_ref[...].astype(jnp.float32)
    block = 64 if rows % 64 == 0 else rows
    for first in range(0, x_ref.shape[1], 128):
        columns = slice(first, first + 128)

        @pl.loop(0, rows // block)
        def _(r):
            base = pl.multiple_of(r * block, block)
            window = padded_ref[pl.ds(base, block + 2 * edge), columns]
            total = jnp.zeros((block, window.shape[1]), jnp.float32)
            for t in range(taps):
                total += taps_ref[t : t + 1, columns] * window[t + shift : t + shift + block]
            active_ref[pl.ds(base, block), columns] = (total / (1.0 + jnp.exp(-total))).astype(
                jnp.bfloat16
            )

    project_refs(active_ref, [weight], sent_ref, kept_ref, product_ref)


def conv_branch(units, taps, blocks, before, after):
    rows, channels = units.shape
    width = blocks[0][0].shape[1]
    arrays, spec = packed(blocks)
    return kernel_call(
        functools.partial(conv_kernel, spec),
        shares(rows, width * len(blocks)),
        (units, before, after, taps, *arrays),
        [
            pltpu.VMEM((rows, width), jnp.float32),
            pltpu.VMEM((rows + 2 * before.shape[0], channels), jnp.float32),
            pltpu.VMEM((rows, channels), jnp.bfloat16),
        ],
    )


def hidden_kernel(spec, halves, mask_ref, *refs):
    weight = unpacked(spec, refs[halves:-2])
    o_ref, x_ref = refs[-2:]
    if halves == 2:
        place_rows(x_ref, refs[0], refs[1])
    else:
        x_ref[...] = refs[0][...]
    rows, width = o_ref.shape
    tile_rows, block = rows // mask_ref.shape[0], width // mask_ref.shape[1]
    tiles, tile = column_tiles(width)

    @pl.loop(0, tiles)
    def _(n):
        units = through(x_ref, weight, pl.ds(pl.multiple_of(n * tile, tile), tile))
        units = units / (1.0 + jnp.exp(-units))
        for r in range(mask_ref.shape[0]):
            for j in range(tile // block):
                masked = (
                    units[r * tile_rows : (r + 1) * tile_rows, j * block : (j + 1) * block]
                    * mask_ref[r, n * (tile // block) + j]
                )
                o_ref[
                    r * tile_rows : (r + 1) * tile_rows,
                    pl.ds(pl.multiple_of(n * tile + j * block, block), block),
                ] = masked.astype(o_ref.dtype)


def hidden_of(rows, weight, mask):
    count = sum(piece.shape[0] for piece in rows)
    arrays, spec = packed(weight)
    return kernel_call(
        functools.partial(hidden_kernel, spec, len(rows)),
        jax.ShapeDtypeStruct((count, arrays[0].shape[1]), jnp.bfloat16),
        (mask, *rows, *arrays),
        [pltpu.VMEM((count, rows[0].shape[1]), jnp.bfloat16)],
        scalars=1,
    )


def on_device(
    residual_in,
    queries,
    keys,
    values,
    w_out,
    conv_value,
    conv_gate,
    depth_kernel,
    conv_out,
    ffn_in,
    ffn_down,
    ffn_mask,
):
    row_count = queries.shape[0]
    count, parts, here = lax.axis_size("seq"), lax.axis_size("dp"), lax.axis_index("dp")
    own_units = ffn_in.shape[1] // parts
    in_columns = lax.dynamic_slice_in_dim(ffn_in, here * own_units, own_units, axis=1)
    down_rows = lax.dynamic_slice_in_dim(ffn_down, here * own_units, own_units, axis=0)
    paired = parts == 2 and lax.axis_size("mp") == 4
    line = Line(3, 1)
    line.add(0, 4, ("value", conv_value), ("gate", conv_gate))
    line.add(1, 5, ("conv_out", conv_out))
    by_head = queries.shape[1] % (count * HEAD_DIM) == 0
    if by_head:
        pieces = heads_by_device(queries, keys, values)
    wide = ffn_down.shape[1]
    last = 128 if wide % (2 * 128) == 0 else wide // 2
    line.add(6, 8, ("down", down_rows[:, wide - last :]), shared=False)
    line.begin()
    weight_out = Gathered(None, w_out, True)

    share_count = row_count // lax.axis_size("mp")
    stream = lax.dynamic_slice_in_dim(
        residual_in, lax.axis_index("mp") * share_count, share_count, 0
    )
    weight_in = Gathered(None, in_columns)
    if by_head:
        pieces, stream = line.visits(1, (pieces, stream))
        pieces = weight_out.cross(pieces)
        pieces = attention_by_head(pieces)
        pieces = [pieces[0]] + [
            lax.ppermute(pieces[d], "seq", [(i, (i - d) % count) for i in range(count)])
            for d in range(1, count)
        ]
        pieces = line.visits(2, pieces)
        pieces = weight_out.end(pieces)
        sent, kept = project_heads(pieces, [weight_out.take()])
    else:
        heads_out = attention(queries, keys, values)
        heads_out = weight_out.end(weight_out.cross(heads_out))
        sent, kept = project(heads_out, [weight_out.take()])
    downs = [Gathered(kept, down_rows[:, : wide - last])]
    kept, taken = fenced(scatter_sum, sent, kept)
    kept, taken = line.visits(2, (kept, taken))
    stream, norm_one = advance(stream, kept, taken, True)
    norm_one = fenced(widen, norm_one)
    norm_one = line.visits(1, norm_one)

    norm_one = line.until(["value", "gate"], norm_one)
    units = gated(norm_one, line.take("value"), line.take("gate"))
    edge = -(-(depth_kernel.shape[0] // 2) // 16) * 16
    up = [(i, i + 1) for i in range(count - 1)]
    before = lax.ppermute(units[row_count - edge :], "seq", up)
    after = lax.ppermute(units[:edge], "seq", [(j, i) for i, j in up])
    units = line.visits(0, units)
    units = line.until(["conv_out"], units)
    sent, kept = conv_branch(units, depth_kernel, line.take("conv_out"), before, after)
    kept, taken = scatter_sum(sent, kept)
    kept, taken = line.visits(2, (kept, taken))
    stream, norm_two = advance(stream, kept, taken, False)

    blocks = ffn_mask.shape[1] // parts
    mask = ffn_mask.astype(jnp.float32)
    if paired:
        rows = rows_of_all(norm_two)
        other = swap(mask, "dp", 1)
        mask = jnp.concatenate(
            [jnp.where(here == 0, mask, other), jnp.where(here == 0, other, mask)], axis=0
        )
    else:
        rows = (lax.all_gather(norm_two, ("dp", "mp"), axis=0, tiled=True),)
        mask = lax.all_gather(mask, "dp", axis=0, tiled=True)
    mask = lax.dynamic_slice_in_dim(mask, here * blocks, blocks, axis=1)
    rows = line.visits(0, rows)
    hidden = hidden_of(rows, weight_in.take(), mask)
    hidden = line.visits(0, hidden)
    pieces = []
    for down in [None, *downs]:
        if down is None:
            hidden = line.until(["down"], hidden)
            sent, kept = project_all(hidden, line.take("down"))
        else:
            if pieces and paired:
                hidden, pieces[-1] = down.end((hidden, pieces[-1]))
            else:
                hidden = down.end(hidden)
            sent, kept = project_all(hidden, down.take())
        if paired:
            pieces.append(sum_over_all(sent, kept))
        else:
            mine = lax.axis_index("mp") % 2
            both = [sent.astype(jnp.float32), kept]
            both = jnp.where(mine == 0, jnp.stack(both[::-1], 2), jnp.stack(both, 2))
            pieces.append(
                (
                    lax.psum_scatter(
                        both.reshape(-1, both.shape[-1]).astype(jnp.bfloat16),
                        ("dp", "mp"),
                        scatter_dimension=0,
                        tiled=True,
                    ),
                )
            )
    return finish(stream, [*pieces[1:], pieces[0]])


def solution(mesh):
    in_specs = (
        P(("dp", "seq"), None),
        P(("dp", "seq"), "mp"),
        P(("dp", "seq"), "mp"),
        P(("dp", "seq"), "mp"),
        P("mp", "seq"),
        P("seq", "mp"),
        P("seq", "mp"),
        P(None, "mp"),
        P("mp", "seq"),
        P("seq", "mp"),
        P("mp", "seq"),
        P(("dp", "seq"), "mp"),
    )
    out_specs = P(("dp", "seq", "mp"), None)
    return jax.shard_map(
        on_device, mesh=mesh, in_specs=in_specs, out_specs=out_specs, check_vma=False
    )
```
